128 devices in a mesh: frame: 32 (over z, y_hi, x), head: 4 (over y_lo, core).
Axes of the slice: x: 4, y: 4 (y_hi: 2, y_lo: 2; y = y_hi * 2 + y_lo), z: 4, core: 2. Of those that a mesh axis runs over, the one named last changes fastest.
Arguments:
- latents: bfloat16 [36864, 3072], P(('frame', 'head')), may hold values from -6 to 6
- mod_shift: float32 [3072], replicated, may hold values from -3 to 3
- mod_scale: float32 [3072], replicated, may hold values from -3 to 3
- mod_gate: float32 [3072], replicated, may hold values from -4 to 4
- packed_weight: bfloat16 [3072, 9216], P(None, 'head'), may hold values from -0.109375 to 0.109375
- query_gain: float32 [128], replicated, may hold values from 0.8 to 2.2
- key_gain: float32 [128], replicated, may hold values from 0.8 to 2.2
- output_weight: bfloat16 [3072, 3072], P('head'), may hold values from -0.109375 to 0.109375
- cached: bfloat16 [36864, 3072], P('frame', 'head'), may hold values from -6 to 6
- active_tiles: int32 [32, 3], P('frame'), may hold values from 0 to 2, as said below
- active_count: int32 [32], P('frame'), may hold values from 1 to 3, as said below
- window_tiles: int32 [32, 3, 5], replicated, may hold values from 0 to 95, as said below
- window_count: int32 [32, 3], P('frame'), may hold values from 1 to 5, as said below
Outputs:
- block_output: bfloat16 [36864, 3072], P(('frame', 'head'))
The draws below stay inside these ranges and needn't reach their ends.
Inputs may be any that keep to these rules, and one draw needn't show every extreme that they name: `active_tiles`: row g lists each of the group's 3 tile numbers once: first the active_count[g] active ones in increasing order, then the others in increasing order. `active_count`: at least one group has all 3 tiles active. `window_tiles`: entry [g, j, w] is a global tile number; the 5 entries of a row are distinct; every entry of group g, padding too, lies in group g - 1, g or g + 1, and over all entries of group g at most 2 distinct tiles of each neighbouring group occur. `window_count`: some live slot uses all 5 entries.
All inputs are finite; a program needn't handle non-finite values.
Results may differ from the reference program's by a relative error of at most 0.01.
Values may be sent and summed in bfloat16 or wider, within the bound.
A program may use at most 128 MiB of HBM per device.

```python
import math
import jax
import jax.numpy as jnp
from jax import lax

D = 3072
HEADS = 24
HD = 128
TILE = 384
WIN = 5
TILES_DEV = 3
RIM = 2
GROUPS = 32
HEADS_DEV = 6
SLAB = 1152
TOKENS = 36864
N_HEAD = 4


def tile_plan(key):
    first_key, second_key, third_key, fourth_key = jax.random.split(key, 4)
    busy_group = jax.random.randint(first_key, (GROUPS,), 0, 4) == 0
    full_group = jax.random.randint(second_key, (), 0, GROUPS)
    light_count = jax.random.randint(third_key, (GROUPS,), 1, max(TILES_DEV // 3, 1) + 1)
    live_count = jnp.where(busy_group | (jnp.arange(GROUPS) == full_group), TILES_DEV, light_count)
    tile_scores = jax.random.randint(fourth_key, (GROUPS, TILES_DEV), 0, 1 << 20) * TILES_DEV + jnp.arange(TILES_DEV)[None, :]
    tile_rank = jnp.argsort(jnp.argsort(tile_scores, axis=1), axis=1)
    chosen = tile_rank < live_count[:, None]
    ordering = jnp.argsort(jnp.where(chosen, 0, TILES_DEV) + jnp.arange(TILES_DEV)[None, :], axis=1)
    return (ordering.astype(jnp.int32), live_count.astype(jnp.int32), full_group)


def draw_active_tiles(key, part):
    return tile_plan(key)[0]


def draw_active_count(key, part):
    return tile_plan(key)[1]


def draw_window_count(key, part):
    full_group = tile_plan(key)[2]
    key = jax.random.fold_in(key, 5)
    counts = jax.random.randint(key, (GROUPS, TILES_DEV), 1, WIN + 1)
    forced = (jnp.arange(GROUPS)[:, None] == full_group) & (jnp.arange(TILES_DEV)[None, :] == 0)
    return jnp.where(forced, WIN, counts).astype(jnp.int32)


def rim_choice(sub_key):
    rim_scores = jax.random.randint(sub_key, (GROUPS, TILES_DEV), 0, 1 << 20) * TILES_DEV + jnp.arange(TILES_DEV)[None, :]
    return jnp.argsort(rim_scores, axis=1)[:, :RIM]


def draw_window_tiles(key, part):
    key = jax.random.fold_in(key, 11)
    left_key, right_key, pick_key = jax.random.split(key, 3)
    group_column = jnp.arange(GROUPS)[:, None]
    own_tiles = group_column * TILES_DEV + jnp.arange(TILES_DEV)[None, :]
    left_tiles = (group_column - 1) * TILES_DEV + rim_choice(left_key)
    right_tiles = (group_column + 1) * TILES_DEV + rim_choice(right_key)
    candidates = jnp.concatenate([own_tiles, left_tiles, right_tiles], axis=1)
    cand_width = TILES_DEV + 2 * RIM
    usable = jnp.concatenate([jnp.ones((GROUPS, TILES_DEV), bool), jnp.broadcast_to(group_column > 0, (GROUPS, RIM)), jnp.broadcast_to(group_column < GROUPS - 1, (GROUPS, RIM))], axis=1)
    pick_scores = jax.random.randint(pick_key, (GROUPS, TILES_DEV, cand_width), 0, 1 << 20) * cand_width + jnp.arange(cand_width)[None, None, :]
    pick_scores = pick_scores + jnp.where(usable[:, None, :], 0, (1 << 20) * cand_width)
    picked = jnp.argsort(pick_scores, axis=2)[:, :, :WIN]
    spread = jnp.broadcast_to(candidates[:, None, :], (GROUPS, TILES_DEV, cand_width))
    return jnp.take_along_axis(spread, picked, axis=2).astype(jnp.int32)


def levels(own_key, extent, pieces, low, top_value):
    loudness, own = 1.0, jax.random.fold_in(own_key, 6)
    for axis_at, parts in pieces:
        heights = jnp.exp(jax.random.uniform(jax.random.fold_in(own, axis_at), (parts,), jnp.float32, low / len(pieces), top_value / len(pieces)))
        loudness = loudness * jnp.repeat(heights, extent[axis_at] // parts).reshape([-1 if axis == axis_at else 1 for axis in range(len(extent))])
    return loudness


def bell_draw(rng, extent, deviation, bound, cuts=(), kind=jnp.bfloat16):
    result = jax.random.normal(rng, extent, jnp.float32) * deviation
    if len(cuts) > 0:
        result = levels(rng, extent, cuts, -0.22, 0.18) * result
    return jnp.clip(result, min=-bound, max=bound).astype(kind)


def setup_inputs(seed: int = 0) -> dict:
    key_of = jax.random.split(jax.random.key(seed), 14)
    return {
        "latents": bell_draw(key_of[0], (TOKENS, D), 1.0, 6.0, ((0, 128),)),
        "mod_shift": bell_draw(key_of[1], (D,), 0.5, 3.0, (), jnp.float32),
        "mod_scale": bell_draw(key_of[2], (D,), 0.5, 3.0, (), jnp.float32),
        "mod_gate": bell_draw(key_of[3], (D,), 1.0, 4.0, (), jnp.float32),
        "packed_weight": bell_draw(key_of[4], (D, 3 * HEADS * HD), D ** -0.5, 0.109375, ((1, 4),)),
        "query_gain": jnp.clip(jax.random.uniform(key_of[5], (HD,), jnp.float32, 0.8, 2.2), 0.8, 2.2),
        "key_gain": jnp.clip(jax.random.uniform(key_of[6], (HD,), jnp.float32, 0.8, 2.2), 0.8, 2.2),
        "output_weight": bell_draw(key_of[7], (HEADS * HD, D), (HEADS * HD) ** -0.5, 0.109375, ((0, 4),)),
        "cached": bell_draw(key_of[8], (TOKENS, HEADS * HD), 1.0, 6.0, ((0, 32), (1, 4))),
        "active_tiles": draw_active_tiles(jax.random.fold_in(key_of[13], 71), 0),
        "active_count": draw_active_count(jax.random.fold_in(key_of[13], 71), 0),
        "window_tiles": draw_window_tiles(jax.random.fold_in(key_of[13], 71), 0),
        "window_count": draw_window_count(jax.random.fold_in(key_of[13], 71), 0),
    }


def modulate(latent_rows, mod_shift, mod_scale):
    widened = latent_rows.astype(jnp.float32)
    centred = widened - lax.optimization_barrier(jnp.mean(widened, axis=-1, keepdims=True))
    variance = lax.optimization_barrier(jnp.mean(centred * centred, axis=-1, keepdims=True))
    return (centred * lax.rsqrt(variance + 1e-06) * (1.0 + mod_scale) + mod_shift).astype(jnp.bfloat16)

def head_norm(vectors, gain_vector):
    mean_square = lax.optimization_barrier(jnp.mean(vectors * vectors, axis=-1, keepdims=True))
    return (vectors * lax.rsqrt(mean_square + 1e-06) * gain_vector).astype(jnp.bfloat16)

def reference(latents, mod_shift, mod_scale, mod_gate, packed_weight, query_gain, key_gain, output_weight, cached, active_tiles, active_count, window_tiles, window_count):
    full_width = HEADS * HD
    grouped = latents.reshape(GROUPS, SLAB, D)

    def project(group_block):
        normed = modulate(group_block, mod_shift, mod_scale)
        packed = jnp.dot(normed, packed_weight, preferred_element_type=jnp.float32).reshape(SLAB, HEADS, 3, HD)
        return (head_norm(packed[:, :, 0], query_gain), head_norm(packed[:, :, 1], key_gain), packed[:, :, 2].astype(jnp.bfloat16))
    queries, keys, values = lax.map(project, grouped)
    key_bank = keys.reshape(GROUPS * TILES_DEV, TILE, HEADS, HD)
    value_bank = values.reshape(GROUPS * TILES_DEV, TILE, HEADS, HD)

    def attend(group_items):
        group_queries, group_cached, group_active, group_live, group_window, group_count = group_items
        slot_queries = group_queries.reshape(TILES_DEV, TILE, HEADS, HD)[group_active]
        slot_keys = key_bank[group_window]
        slot_values = value_bank[group_window]
        scores = jnp.einsum('jqhd,jwkhd->jhqwk', slot_queries.astype(jnp.float32), slot_keys.astype(jnp.float32)) / math.sqrt(HD)
        inside = jnp.arange(WIN, dtype=jnp.int32)[None, :] < group_count[:, None]
        weights = jnp.where(inside[:, None, None, :, None], jnp.exp(scores), 0.0)
        totals = lax.optimization_barrier(jnp.sum(weights, axis=(3, 4)))
        rounded = lax.optimization_barrier(weights.astype(jnp.bfloat16)).astype(jnp.float32)
        numerator = jnp.einsum('jhqwk,jwkhd->jqhd', rounded, slot_values.astype(jnp.float32))
        slot_out = (numerator / jnp.transpose(totals, (0, 2, 1))[..., None]).astype(jnp.bfloat16)
        tile_ids = jnp.arange(TILES_DEV, dtype=jnp.int32)
        placement = (group_active[:, None] == tile_ids[None, :]) & (tile_ids < group_live)[:, None]
        placed = jnp.einsum('jt,jqc->tqc', placement.astype(jnp.float32), slot_out.reshape(TILES_DEV, TILE, full_width).astype(jnp.float32))
        is_active = jnp.any(placement, axis=0)
        cached_tiles = group_cached.reshape(TILES_DEV, TILE, full_width).astype(jnp.float32)
        merged = jnp.where(is_active[:, None, None], placed, cached_tiles).astype(jnp.bfloat16)
        return merged.reshape(SLAB, full_width)
    attended = lax.map(attend, (queries, cached.reshape(GROUPS, SLAB, full_width), active_tiles, active_count, window_tiles, window_count))
    share_width = HEADS_DEV * HD

    def finish(group_items):
        group_attended, group_latents = group_items
        summed = jnp.zeros((SLAB, D), jnp.float32)
        for head_group in range(N_HEAD):
            partial_out = jnp.dot(group_attended[:, head_group * share_width:(head_group + 1) * share_width], output_weight[head_group * share_width:(head_group + 1) * share_width], preferred_element_type=jnp.float32)
            summed = summed + lax.optimization_barrier(partial_out.astype(jnp.bfloat16)).astype(jnp.float32)
        return (group_latents.astype(jnp.float32) + mod_gate * summed).astype(jnp.bfloat16)
    return lax.map(finish, (attended, grouped)).reshape(TOKENS, D)
```

```python
import functools
import math

import jax
import jax.numpy as jnp
from jax import lax
from jax.experimental import pallas as pl
from jax.experimental.pallas import tpu as pltpu
from jax.sharding import PartitionSpec as P

HD = 128
BF16 = jnp.bfloat16
F32 = jnp.float32
MESH = pl.DeviceIdType.MESH


def kernel(
    sizes,
    latents_hbm,
    shift_ref,
    scale_ref,
    gate_ref,
    weight_hbm,
    query_gain_ref,
    key_gain_ref,
    out_weight_hbm,
    cached_hbm,
    active_tiles_ref,
    active_count_ref,
    window_tiles_ref,
    window_count_ref,
    out_hbm,
    latents,
    near,
    far,
    weight,
    queries,
    bank,
    rim_send,
    rim,
    numerator,
    totals,
    attended,
    out_weight,
    sib_sums,
    cross_sums,
    masks,
    local_sem,
    near_sib_send,
    near_sib_recv,
    cross_send,
    cross_recv,
    pass_send,
    pass_recv,
    rim_send_sem,
    rim_recv_sem,
    sums_send,
    sums_recv,
    last_send,
    last_recv,
):
    groups, heads, tile, width, window = sizes
    share = heads * HD
    chunk = tile // 4
    rows = 3 * chunk
    g = lax.axis_index("frame")
    h = lax.axis_index("head")
    y = h // 2
    c = h % 2
    sibling = y * 2 + (1 - c)
    cross = (1 - y) * 2 + c
    right = (g + 1) % groups
    left = (g + groups - 1) % groups

    def aligned(start):
        return pl.multiple_of(start, chunk)

    load_latents = pltpu.make_async_copy(latents_hbm, latents, local_sem.at[0])
    load_latents.start()
    parts = 3
    part_width = 3 * share // parts
    load_weight = [
        pltpu.make_async_copy(
            weight_hbm.at[:, pl.ds(part * part_width, part_width)],
            weight.at[:, pl.ds(part * part_width, part_width)],
            local_sem.at[1 + part],
        )
        for part in range(parts)
    ]
    for load in load_weight:
        load.start()
    load_out_weight = pltpu.make_async_copy(out_weight_hbm, out_weight, local_sem.at[4])
    load_cached = pltpu.make_async_copy(cached_hbm, attended, local_sem.at[5])

    barrier = pltpu.get_barrier_semaphore()
    for partner in ((g, sibling), (g, cross), (left, h), (right, h)):
        pl.semaphore_signal(barrier, inc=1, device_id=partner, device_id_type=MESH)
    pl.semaphore_wait(barrier, 4)

    load_latents.wait()
    to_sibling, to_cross = [], []
    for step in range(3):
        mine = (1 - y) * (2 - step) + y * step
        x = latents[pl.ds(aligned(mine * chunk), chunk), :].astype(F32)
        centred = x - jnp.mean(x, axis=-1, keepdims=True)
        variance = jnp.mean(centred * centred, axis=-1, keepdims=True)
        normed = (
            centred * lax.rsqrt(variance + 1e-06) * (1.0 + scale_ref[...]) + shift_ref[...]
        ).astype(BF16)
        place = aligned(c * rows + mine * chunk)
        near[pl.ds(place, chunk), :] = normed
        over = pltpu.make_async_remote_copy(
            src_ref=near.at[pl.ds(place, chunk), :],
            dst_ref=far.at[step, pl.ds(aligned(c * chunk), chunk), :],
            send_sem=cross_send.at[step],
            recv_sem=cross_recv.at[step],
            device_id=(g, cross),
            device_id_type=MESH,
        )
        over.start()
        to_cross.append(over)
        beside = pltpu.make_async_remote_copy(
            src_ref=near.at[pl.ds(place, chunk), :],
            dst_ref=near.at[pl.ds(place, chunk), :],
            send_sem=near_sib_send.at[step],
            recv_sem=near_sib_recv.at[step],
            device_id=(g, sibling),
            device_id_type=MESH,
        )
        beside.start()
        to_sibling.append(beside)

    def rim_tiles(reader, owner):
        used = [jnp.int32(0)] * 3
        for j in range(3):
            for w in range(window):
                entry = window_tiles_ref[reader, j, w]
                for t in range(3):
                    used[t] = used[t] | (entry == owner * 3 + t).astype(jnp.int32)
        spare = jnp.where(used[1] == 0, 1, jnp.where(used[0] == 0, 0, 2))
        return jnp.where(spare == 0, 1, 0), jnp.where(spare == 2, 1, 2)

    send_tiles = [rim_tiles(right, g), rim_tiles(left, g)]
    recv_tiles = [rim_tiles(g, left), rim_tiles(g, right)]
    candidates = [g * 3, g * 3 + 1, g * 3 + 2]
    for side, owner in ((0, left), (1, right)):
        candidates += [owner * 3 + recv_tiles[side][0], owner * 3 + recv_tiles[side][1]]
    named = []
    for j in range(3):
        hits = [jnp.int32(0)] * 7
        for w in range(window):
            entry = window_tiles_ref[g, j, w]
            inside = (w < window_count_ref[0, j]).astype(jnp.int32)
            for k in range(7):
                hits[k] = hits[k] + inside * (entry == candidates[k]).astype(jnp.int32)
        named.append(hits)
    for t in range(3):
        holds = [
            ((active_tiles_ref[0, j] == t) & (j < active_count_ref[0])).astype(jnp.int32)
            for j in range(3)
        ]
        for k in range(7):
            masks[t * 8 + k] = sum(holds[j] * named[j][k] for j in range(3)).astype(F32)
        masks[t * 8 + 7] = sum(holds).astype(F32)

    def head_norm(vectors, gain_ref):
        mean_square = jnp.mean(vectors * vectors, axis=-1, keepdims=True)
        return (vectors * lax.rsqrt(mean_square + 1e-06) * gain_ref[...]).astype(BF16)

    pair = 2 * 3 * HD

    def project(block, places):
        def body(step, carry):
            columns = pl.ds(pl.multiple_of(step * pair, pair), pair)
            packed = jnp.dot(block[...], weight[:, columns], preferred_element_type=F32)
            for half in range(2):
                at = half * 3 * HD
                head = step * 2 + half
                query_columns = pl.ds(pl.multiple_of(head * HD, HD), HD)
                value_columns = pl.ds(pl.multiple_of(share + head * HD, HD), HD)
                q = head_norm(packed[:, at : at + HD], query_gain_ref)
                k = head_norm(packed[:, at + HD : at + 2 * HD], key_gain_ref)
                v = packed[:, at + 2 * HD : at + 3 * HD].astype(BF16)
                for first, place, count in places:
                    queries[pl.ds(place, count), query_columns] = q[first : first + count]
                    bank[pl.ds(place, count), query_columns] = k[first : first + count]
                    bank[pl.ds(place, count), value_columns] = v[first : first + count]
            return carry

        lax.fori_loop(0, heads // 2, body, 0)

    order = ((0, 0), (0, 1), (0, 2), (1, 1), (0, 3), (1, 2), (1, 0), (1, 3))
    rim_copies = {}

    def send_rim(slot):
        second, quarter = order[slot]
        second = second + y * (1 - 2 * second)
        quarter = quarter + y * (3 - 2 * quarter)
        base = aligned((4 * second + quarter) * chunk)
        other = aligned((4 * second + quarter + 4) * chunk)
        low = bank[pl.ds(base, chunk), :]
        high = bank[pl.ds(other, chunk), :]
        for side in range(2):
            first_tile, second_tile = send_tiles[side]
            takes_high = jnp.where(second == 0, first_tile - 0, second_tile - 1)
            rim_send[side, slot] = jnp.where(takes_high == 1, high, low)
            copy = pltpu.make_async_remote_copy(
                src_ref=rim_send.at[side, slot],
                dst_ref=rim.at[side, second, pl.ds(aligned(quarter * chunk), chunk), :],
                send_sem=rim_send_sem.at[side, slot],
                recv_sem=rim_recv_sem.at[side, slot],
                device_id=(right if side == 0 else left, h),
                device_id_type=MESH,
            )
            copy.start()
            rim_copies[side, slot] = copy

    for load in load_weight:
        load.wait()
    load_out_weight.start()
    load_cached.start()
    for copy in to_sibling:
        copy.wait_recv()
    project(near, [(0, aligned(y * 2 * rows), 2 * rows)])
    send_rim(0)
    send_rim(1)
    passed = []
    for step in range(3):
        to_cross[step].wait_recv()
        onward = pltpu.make_async_remote_copy(
            src_ref=far.at[step, pl.ds(aligned(c * chunk), chunk), :],
            dst_ref=far.at[step, pl.ds(aligned(c * chunk), chunk), :],
            send_sem=pass_send.at[step],
            recv_sem=pass_recv.at[step],
            device_id=(g, sibling),
            device_id_type=MESH,
        )
        onward.start()
        passed.append(onward)
        onward.wait_recv()
        theirs = y * (2 - step) + (1 - y) * step
        start = (1 - y) * 2 * rows + theirs * chunk
        project(
            far.at[step],
            [(0, aligned(start), chunk), (chunk, aligned(start + rows), chunk)],
        )
        send_rim(2 * step + 2)
        send_rim(2 * step + 3)

    log_scale = math.log2(math.e) / math.sqrt(HD)

    def one_pair(q, k, v, mask):
        scores = lax.dot_general(q, k, (((1,), (1,)), ((), ())), preferred_element_type=F32)
        weights = jnp.exp2(scores * log_scale)
        folded = weights[:, :HD] if tile >= HD else jnp.pad(weights, ((0, 0), (0, HD - tile)))
        for at in range(HD, tile, HD):
            folded = folded + weights[:, at : at + HD]
        out = jnp.dot(weights.astype(BF16), v, preferred_element_type=F32)
        return out * mask, folded * mask

    def own_body(index, carry):
        t = index // heads
        head = index % heads
        here = pl.ds(aligned(t * tile), tile)
        columns = pl.ds(pl.multiple_of(head * HD, HD), HD)
        value_columns = pl.ds(pl.multiple_of(share + head * HD, HD), HD)
        q = queries[here, columns]
        out, total = None, None
        for k in range(3):
            there = pl.ds(k * tile, tile)
            more_out, more_total = one_pair(
                q, bank[there, columns], bank[there, value_columns], masks[t * 8 + k]
            )
            out = more_out if out is None else out + more_out
            total = more_total if total is None else total + more_total
        numerator[here, columns] = out
        totals[here, columns] = total
        return carry

    lax.fori_loop(0, 3 * heads, own_body, 0)

    def rim_sum(t, head, second):
        here = pl.ds(aligned(t * tile), tile)
        columns = pl.ds(pl.multiple_of(head * HD, HD), HD)
        value_columns = pl.ds(pl.multiple_of(share + head * HD, HD), HD)
        q = queries[here, columns]
        out, total = numerator[here, columns], totals[here, columns]
        for side in range(2):
            more_out, more_total = one_pair(
                q,
                rim[side, second, :, columns],
                rim[side, second, :, value_columns],
                masks[t * 8 + 3 + 2 * side + second],
            )
            out, total = out + more_out, total + more_total
        return here, columns, out, total

    def first_rim_body(index, carry):
        here, columns, out, total = rim_sum(index // heads, index % heads, y)
        numerator[here, columns] = out
        totals[here, columns] = total
        return carry

    def second_rim_tile(t):
        def body(head, carry):
            here, columns, out, total = rim_sum(t, head, 1 - y)
            slot_out = (out / jnp.sum(total, axis=-1, keepdims=True)).astype(BF16)
            attended[here, columns] = jnp.where(
                masks[t * 8 + 7] > 0.5, slot_out, attended[here, columns]
            )
            return carry

        lax.fori_loop(0, heads, body, 0)

    for slot in (0, 1, 2, 4):
        for side in range(2):
            rim_copies[side, slot].wait_recv()
    lax.fori_loop(0, 3 * heads, first_rim_body, 0)

    load_out_weight.wait()
    load_cached.wait()
    for copies in (to_sibling, to_cross, passed):
        for copy in copies:
            copy.wait_send()
    for slot in (3, 5, 6, 7):
        for side in range(2):
            rim_copies[side, slot].wait_recv()
    second_rim_tile((1 - y) * 2)
    second_rim_tile(1)

    def partial_sums(first, second):
        both = jnp.concatenate(
            [attended[pl.ds(aligned(first), chunk), :], attended[pl.ds(aligned(second), chunk), :]],
            axis=0,
        )
        return jnp.dot(both, out_weight[...], preferred_element_type=F32).astype(BF16)

    sums = []

    def project_out(slot, step, chip, chunk_at):
        owner = chip * 2 * rows + chunk_at * chunk
        both = partial_sums(owner + c * rows, owner + (1 - c) * rows)
        half = slot // 3
        near[pl.ds(half * rows + step * chunk, chunk), :] = both[:chunk]
        far[step, pl.ds(half * chunk, chunk), :] = both[chunk:]
        copy = pltpu.make_async_remote_copy(
            src_ref=far.at[step, pl.ds(half * chunk, chunk), :],
            dst_ref=sib_sums.at[slot],
            send_sem=sums_send.at[slot],
            recv_sem=sums_recv.at[slot],
            device_id=(g, sibling),
            device_id_type=MESH,
        )
        copy.start()
        sums.append(copy)

    last = []

    def send_last(step):
        sums[step].wait_recv()
        kept = near[pl.ds(step * chunk, chunk), :].astype(F32)
        near[pl.ds(step * chunk, chunk), :] = (kept + sib_sums[step].astype(F32)).astype(BF16)
        copy = pltpu.make_async_remote_copy(
            src_ref=near.at[pl.ds(step * chunk, chunk), :],
            dst_ref=cross_sums.at[step],
            send_sem=last_send.at[step],
            recv_sem=last_recv.at[step],
            device_id=(g, cross),
            device_id_type=MESH,
        )
        copy.start()
        last.append(copy)

    for step in range(3):
        project_out(step, step, 1 - y, step)
        if step > 0:
            send_last(step - 1)
    send_last(2)
    second_rim_tile(y * 2)
    for step in range(3):
        project_out(3 + step, step, y, step)
    stores = []
    for step in range(3):
        sums[3 + step].wait_recv()
        last[step].wait_recv()
        here = pl.ds(step * chunk, chunk)
        total = (
            near[pl.ds(rows + step * chunk, chunk), :].astype(F32)
            + sib_sums[3 + step].astype(F32)
            + cross_sums[step].astype(F32)
        )
        latents[here, :] = (latents[here, :].astype(F32) + gate_ref[...] * total).astype(BF16)
        store = pltpu.make_async_copy(
            latents.at[here, :], out_hbm.at[here, :], local_sem.at[step]
        )
        store.start()
        stores.append(store)
    for store in stores:
        store.wait()
    for copies in (sums, last, rim_copies.values()):
        for copy in copies:
            copy.wait_send()


def on_device(
    latents,
    mod_shift,
    mod_scale,
    mod_gate,
    packed_weight,
    query_gain,
    key_gain,
    output_weight,
    cached,
    active_tiles,
    active_count,
    window_tiles,
    window_count,
):
    rows, width = latents.shape
    groups, tiles, window = window_tiles.shape
    share = cached.shape[1]
    heads = share // HD
    slab = cached.shape[0]
    tile = slab // tiles
    chunk = tile // 4
    assert tiles == 3 and rows == 3 * chunk and slab == 4 * rows
    anywhere = pl.BlockSpec(memory_space=pl.ANY)
    vmem = pl.BlockSpec(memory_space=pltpu.VMEM)
    smem = pl.BlockSpec(memory_space=pltpu.SMEM)
    dma = pltpu.SemaphoreType.DMA
    return pl.pallas_call(
        functools.partial(kernel, (groups, heads, tile, width, window)),
        out_shape=jax.ShapeDtypeStruct((rows, width), BF16),
        in_specs=[
            anywhere,
            vmem,
            vmem,
            vmem,
            anywhere,
            vmem,
            vmem,
            anywhere,
            anywhere,
            smem,
            smem,
            smem,
            smem,
        ],
        out_specs=anywhere,
        scratch_shapes=[
            pltpu.VMEM((rows, width), BF16),
            pltpu.VMEM((2 * rows, width), BF16),
            pltpu.VMEM((3, 2 * chunk, width), BF16),
            pltpu.VMEM((width, 3 * share), BF16),
            pltpu.VMEM((slab, share), BF16),
            pltpu.VMEM((slab, 2 * share), BF16),
            pltpu.VMEM((2, 8, chunk, 2 * share), BF16),
            pltpu.VMEM((2, 2, tile, 2 * share), BF16),
            pltpu.VMEM((slab, share), F32),
            pltpu.VMEM((slab, share), F32),
            pltpu.VMEM((slab, share), BF16),
            pltpu.VMEM((share, width), BF16),
            pltpu.VMEM((6, chunk, width), BF16),
            pltpu.VMEM((3, chunk, width), BF16),
            pltpu.SMEM((24,), F32),
            dma((6,)),
            dma((3,)),
            dma((3,)),
            dma((3,)),
            dma((3,)),
            dma((3,)),
            dma((3,)),
            dma((2, 8)),
            dma((2, 8)),
            dma((6,)),
            dma((6,)),
            dma((3,)),
            dma((3,)),
        ],
        compiler_params=pltpu.CompilerParams(
            collective_id=0, has_side_effects=True, vmem_limit_bytes=VMEM_LIMIT
        ),
    )(
        latents,
        mod_shift[None],
        mod_scale[None],
        mod_gate[None],
        packed_weight,
        query_gain[None],
        key_gain[None],
        output_weight,
        cached,
        active_tiles,
        active_count,
        window_tiles,
        window_count,
    )


VMEM_LIMIT = 64 * 1024 * 1024


def solution(mesh):
    in_specs = (
        P(("frame", "head"), None),
        P(),
        P(),
        P(),
        P(None, "head"),
        P(),
        P(),
        P("head", None),
        P("frame", "head"),
        P("frame", None),
        P("frame"),
        P(),
        P("frame", None),
    )
    return jax.shard_map(
        on_device,
        mesh=mesh,
        in_specs=in_specs,
        out_specs=P(("frame", "head"), None),
        check_vma=False,
    )
```

```python
import functools
import math

import jax
import jax.numpy as jnp
from jax import lax
from jax.experimental import pallas as pl
from jax.experimental.pallas import tpu as pltpu
from jax.sharding import PartitionSpec as P

HD = 128
ROW = 4
BF16 = jnp.bfloat16
F32 = jnp.float32
MESH = pl.DeviceIdType.MESH


def kernel(
    sizes,
    latents_hbm,
    shift_ref,
    scale_ref,
    gate_ref,
    weight_hbm,
    query_gain_ref,
    key_gain_ref,
    out_weight_hbm,
    cached_hbm,
    active_tiles_ref,
    active_count_ref,
    window_tiles_ref,
    window_count_ref,
    out_hbm,
    latents,
    rows_buffer,
    weight,
    queries,
    bank,
    rim_send,
    rim,
    rim_rows,
    numerator,
    totals,
    attended,
    out_weight,
    cross_sums,
    masks,
    local_sem,
    near_sib_send,
    near_sib_recv,
    cross_send,
    cross_recv,
    pass_send,
    pass_recv,
    rim_send_sem,
    rim_recv_sem,
    rim_pass_send,
    rim_pass_recv,
    sums_send,
    sums_recv,
    last_send,
    last_recv,
    free_sem,
):
    groups, heads, tile, width, window = sizes
    share = heads * HD
    chunk = tile // 4
    rows = 3 * chunk
    g = lax.axis_index("frame")
    h = lax.axis_index("head")
    y = h // 2
    c = h % 2
    sibling = y * 2 + (1 - c)
    cross = (1 - y) * 2 + c
    right = (g + 1) % groups
    left = (g + groups - 1) % groups
    left_edge = (ROW - g % ROW) // ROW
    right_edge = (g % ROW + 1) // ROW
    left_partner = (left, h + left_edge * (cross - h))
    right_partner = (right, h + right_edge * (cross - h))
    edge_side = right_edge

    def aligned(start):
        return pl.multiple_of(start, chunk)

    def far_place(step, core):
        return aligned((6 + 2 * step + core) * chunk)

    load_latents = pltpu.make_async_copy(latents_hbm, latents, local_sem.at[0])
    load_latents.start()
    parts = 3
    part_width = 3 * share // parts
    load_weight = [
        pltpu.make_async_copy(
            weight_hbm.at[:, pl.ds(part * part_width, part_width)],
            weight.at[:, pl.ds(part * part_width, part_width)],
            local_sem.at[1 + part],
        )
        for part in range(parts)
    ]
    for load in load_weight:
        load.start()
    load_out_weight = pltpu.make_async_copy(out_weight_hbm, out_weight, local_sem.at[4])
    load_cached = pltpu.make_async_copy(cached_hbm, attended, local_sem.at[5])

    barrier = pltpu.get_barrier_semaphore()
    for partner in ((g, sibling), (g, cross), left_partner, right_partner):
        pl.semaphore_signal(barrier, inc=1, device_id=partner, device_id_type=MESH)
    pl.semaphore_wait(barrier, 4)

    load_latents.wait()
    to_sibling, to_cross = [], []
    for step in range(3):
        mine = (1 - y) * (2 - step) + y * step
        x = latents[pl.ds(aligned(mine * chunk), chunk), :].astype(F32)
        centred = x - jnp.mean(x, axis=-1, keepdims=True)
        variance = jnp.mean(centred * centred, axis=-1, keepdims=True)
        normed = (
            centred * lax.rsqrt(variance + 1e-06) * (1.0 + scale_ref[...]) + shift_ref[...]
        ).astype(BF16)
        place = aligned(c * rows + mine * chunk)
        rows_buffer[pl.ds(place, chunk), :] = normed
        over = pltpu.make_async_remote_copy(
            src_ref=rows_buffer.at[pl.ds(place, chunk), :],
            dst_ref=rows_buffer.at[pl.ds(far_place(step, c), chunk), :],
            send_sem=cross_send.at[step],
            recv_sem=cross_recv.at[step],
            device_id=(g, cross),
            device_id_type=MESH,
        )
        over.start()
        to_cross.append(over)
        beside = pltpu.make_async_remote_copy(
            src_ref=rows_buffer.at[pl.ds(place, chunk), :],
            dst_ref=rows_buffer.at[pl.ds(place, chunk), :],
            send_sem=near_sib_send.at[step],
            recv_sem=near_sib_recv.at[step],
            device_id=(g, sibling),
            device_id_type=MESH,
        )
        beside.start()
        to_sibling.append(beside)

    def rim_tiles(reader, owner):
        used = [jnp.int32(0)] * 3
        for j in range(3):
            for w in range(window):
                entry = window_tiles_ref[reader, j, w]
                for t in range(3):
                    used[t] = used[t] | (entry == owner * 3 + t).astype(jnp.int32)
        spare = jnp.where(used[1] == 0, 1, jnp.where(used[0] == 0, 0, 2))
        return jnp.where(spare == 0, 1, 0), jnp.where(spare == 2, 1, 2)

    send_tiles = [rim_tiles(right, g), rim_tiles(left, g)]
    recv_tiles = [rim_tiles(g, left), rim_tiles(g, right)]
    candidates = [g * 3, g * 3 + 1, g * 3 + 2]
    for side, owner in ((0, left), (1, right)):
        candidates += [owner * 3 + recv_tiles[side][0], owner * 3 + recv_tiles[side][1]]
    named = []
    for j in range(3):
        hits = [jnp.int32(0)] * 7
        for w in range(window):
            entry = window_tiles_ref[g, j, w]
            inside = (w < window_count_ref[0, j]).astype(jnp.int32)
            for k in range(7):
                hits[k] = hits[k] + inside * (entry == candidates[k]).astype(jnp.int32)
        named.append(hits)
    for t in range(3):
        holds = [
            ((active_tiles_ref[0, j] == t) & (j < active_count_ref[0])).astype(jnp.int32)
            for j in range(3)
        ]
        for k in range(7):
            masks[t * 8 + k] = sum(holds[j] * named[j][k] for j in range(3)).astype(F32)
        masks[t * 8 + 7] = sum(holds).astype(F32)

    def head_norm(vectors, gain_ref):
        mean_square = jnp.mean(vectors * vectors, axis=-1, keepdims=True)
        return (vectors * lax.rsqrt(mean_square + 1e-06) * gain_ref[...]).astype(BF16)

    pair = 2 * 3 * HD

    def project(block_at, places):
        def body(step, carry):
            columns = pl.ds(pl.multiple_of(step * pair, pair), pair)
            packed = jnp.dot(rows_buffer[block_at, :], weight[:, columns], preferred_element_type=F32)
            for half in range(2):
                at = half * 3 * HD
                head = step * 2 + half
                query_columns = pl.ds(pl.multiple_of(head * HD, HD), HD)
                value_columns = pl.ds(pl.multiple_of(share + head * HD, HD), HD)
                q = head_norm(packed[:, at : at + HD], query_gain_ref)
                k = head_norm(packed[:, at + HD : at + 2 * HD], key_gain_ref)
                v = packed[:, at + 2 * HD : at + 3 * HD].astype(BF16)
                for first, place, count in places:
                    queries[pl.ds(place, count), query_columns] = q[first : first + count]
                    bank[pl.ds(place, count), query_columns] = k[first : first + count]
                    bank[pl.ds(place, count), value_columns] = v[first : first + count]
            return carry

        lax.fori_loop(0, heads // 2, body, 0)

    order = ((0, 0), (0, 1), (0, 2), (1, 1), (0, 3), (1, 2), (1, 0), (1, 3))

    def quarter_of(slot, chip):
        second, quarter = order[slot]
        return second + chip * (1 - 2 * second), quarter + chip * (3 - 2 * quarter)

    def row_place(piece):
        chip, inside = piece // 6, piece % 6
        away = (chip + y) % 2
        number = inside % 3
        step = y * (2 - number) + (1 - y) * number
        return aligned(
            (1 - away) * inside * chunk + away * (6 + 2 * step + inside // 3) * chunk
        )

    half_width = width // 2

    def tile_copy(side, slot):
        second, quarter = quarter_of(slot, y)
        return pltpu.make_async_remote_copy(
            src_ref=rim_send.at[side, slot],
            dst_ref=rim.at[side, second, pl.ds(aligned(quarter * chunk), chunk), :],
            send_sem=rim_send_sem.at[side, slot],
            recv_sem=rim_recv_sem.at[side, slot],
            device_id=(right if side == 0 else left, h),
            device_id_type=MESH,
        )

    def edge_copy(side, slot):
        stage, half = slot // 2, slot % 2
        target = left + (1 - side) * (right - left)
        return pltpu.make_async_remote_copy(
            src_ref=rim_send.at[side, slot],
            dst_ref=rim_rows.at[
                pl.ds(aligned((2 * stage + c) * chunk), chunk),
                pl.ds(half * half_width, half_width),
            ],
            send_sem=rim_send_sem.at[side, slot],
            recv_sem=rim_recv_sem.at[side, slot],
            device_id=(target, cross),
            device_id_type=MESH,
        )

    def edge_pass(stage):
        here = pl.ds(aligned((2 * stage + c) * chunk), chunk)
        return pltpu.make_async_remote_copy(
            src_ref=rim_rows.at[here, :],
            dst_ref=rim_rows.at[here, :],
            send_sem=rim_pass_send.at[stage],
            recv_sem=rim_pass_recv.at[stage],
            device_id=(g, sibling),
            device_id_type=MESH,
        )

    def takes_high(side, second):
        first_tile, second_tile = send_tiles[side]
        return jnp.where(second == 0, first_tile, second_tile - 1) == 1

    def send_rim(stage):
        for side in range(2):
            edge = right_edge if side == 0 else left_edge

            @pl.when(edge == 0)
            def _():
                for slot in (2 * stage, 2 * stage + 1):
                    second, quarter = quarter_of(slot, y)
                    low = bank[pl.ds(aligned((4 * second + quarter) * chunk), chunk), :]
                    high = bank[pl.ds(aligned((4 * second + quarter + 4) * chunk), chunk), :]
                    rim_send[side, slot] = jnp.where(takes_high(side, second), high, low)
                    tile_copy(side, slot).start()

            @pl.when(edge == 1)
            def _():
                second, quarter = (
                    (1 - c) * even + c * odd
                    for even, odd in zip(quarter_of(2 * stage, y), quarter_of(2 * stage + 1, y))
                )
                low = row_place(4 * second + quarter)
                high = row_place(4 * second + quarter + 4)
                for half in range(2):
                    columns = pl.ds(half * half_width, half_width)
                    rim_send[side, 2 * stage + half] = jnp.where(
                        takes_high(side, second),
                        rows_buffer[pl.ds(high, chunk), columns],
                        rows_buffer[pl.ds(low, chunk), columns],
                    )
                    edge_copy(side, 2 * stage + half).start()

    def wait_rim(slots):
        for side in range(2):
            edge = left_edge if side == 0 else right_edge

            @pl.when(edge == 0)
            def _():
                for slot in slots:
                    tile_copy(side, slot).wait_recv()

    def edge_stages(stages):
        @pl.when(left_edge + right_edge == 1)
        def _():
            for stage in stages:
                for half in range(2):
                    edge_copy(edge_side, 2 * stage + half).wait_recv()
                edge_pass(stage).start()
            for stage in stages:
                edge_pass(stage).wait_recv()
                places = []
                for core in range(2):
                    second, quarter = quarter_of(2 * stage + core, 1 - y)
                    places.append((core * chunk, second, aligned(quarter * chunk)))

                def body(head, carry):
                    columns = pl.ds(pl.multiple_of(head * 3 * HD + HD, HD), 2 * HD)
                    packed = jnp.dot(
                        rim_rows[pl.ds(2 * stage * chunk, 2 * chunk), :],
                        weight[:, columns],
                        preferred_element_type=F32,
                    )
                    k = head_norm(packed[:, :HD], key_gain_ref)
                    v = packed[:, HD:].astype(BF16)
                    key_columns = pl.ds(pl.multiple_of(head * HD, HD), HD)
                    value_columns = pl.ds(pl.multiple_of(share + head * HD, HD), HD)
                    for first, second, place in places:
                        there = pl.ds(place, chunk)
                        rim[edge_side, second, there, key_columns] = k[first : first + chunk]
                        rim[edge_side, second, there, value_columns] = v[first : first + chunk]
                    return carry

                lax.fori_loop(0, heads, body, 0)

    log_scale = math.log2(math.e) / math.sqrt(HD)
    near_tile = y * 2
    far_tile = (1 - y) * 2

    def attend(q, keys, values, names):
        result = None
        for k, v, name in zip(keys, values, names):
            scores = lax.dot_general(
                q, k, (((1,), (1,)), ((), ())), preferred_element_type=F32
            )
            weights = jnp.exp2(scores * log_scale).astype(BF16)
            both = jnp.concatenate([v, jnp.ones_like(v)], axis=1)
            both = jnp.where(name > 0.5, both, jnp.zeros_like(both))
            out = jnp.dot(weights, both, preferred_element_type=F32)
            result = out if result is None else result + out
        return result[:, :HD], result[:, HD:]

    def own_pairs(t, others, first):
        def body(head, carry):
            here = pl.ds(aligned(t * tile), tile)
            columns = pl.ds(pl.multiple_of(head * HD, HD), HD)
            value_columns = pl.ds(pl.multiple_of(share + head * HD, HD), HD)
            there = [pl.ds(aligned(other * tile), tile) for other in others]
            out, total = attend(
                queries[here, columns],
                [bank[place, columns] for place in there],
                [bank[place, value_columns] for place in there],
                [masks[t * 8 + other] for other in others],
            )
            if not first:
                out, total = numerator[here, columns] + out, totals[here, columns] + total
            numerator[here, columns] = out
            totals[here, columns] = total
            return carry

        lax.fori_loop(0, heads, body, 0)

    for load in load_weight:
        load.wait()
    load_out_weight.start()
    load_cached.start()
    for copy in to_sibling:
        copy.wait_recv()
    project(pl.ds(0, 2 * rows), [(0, aligned(y * 2 * rows), 2 * rows)])
    send_rim(0)
    passed = []
    for step in range(3):
        to_cross[step].wait_recv()
        onward = pltpu.make_async_remote_copy(
            src_ref=rows_buffer.at[pl.ds(far_place(step, c), chunk), :],
            dst_ref=rows_buffer.at[pl.ds(far_place(step, c), chunk), :],
            send_sem=pass_send.at[step],
            recv_sem=pass_recv.at[step],
            device_id=(g, sibling),
            device_id_type=MESH,
        )
        onward.start()
        passed.append(onward)
        onward.wait_recv()
        theirs = y * (2 - step) + (1 - y) * step
        start = (1 - y) * 2 * rows + theirs * chunk
        project(
            pl.ds(far_place(step, 0), 2 * chunk),
            [(0, aligned(start), chunk), (chunk, aligned(start + rows), chunk)],
        )
        send_rim(step + 1)
        if step == 0:
            own_pairs(near_tile, [near_tile], True)
        if step == 1:
            own_pairs(near_tile, [1], False)
            own_pairs(1, [near_tile, 1], True)
    own_pairs(near_tile, [far_tile], False)
    own_pairs(1, [far_tile], False)
    own_pairs(far_tile, [near_tile, 1, far_tile], True)

    def rim_sum(t, head, phase):
        here = pl.ds(aligned(t * tile), tile)
        columns = pl.ds(pl.multiple_of(head * HD, HD), HD)
        value_columns = pl.ds(pl.multiple_of(share + head * HD, HD), HD)
        keys, values, names = [], [], []
        for side in range(2):
            edge = left_edge if side == 0 else right_edge
            second = (y + edge + phase) % 2
            keys.append(rim[side, second, :, columns])
            values.append(rim[side, second, :, value_columns])
            names.append(masks[t * 8 + 3 + 2 * side + second])
        out, total = attend(queries[here, columns], keys, values, names)
        return here, columns, numerator[here, columns] + out, totals[here, columns] + total

    def first_rim_body(index, carry):
        here, columns, out, total = rim_sum(index // heads, index % heads, 0)
        numerator[here, columns] = out
        totals[here, columns] = total
        return carry

    def second_rim_tile(t):
        def body(head, carry):
            here, columns, out, total = rim_sum(t, head, 1)
            slot_out = (out / total).astype(BF16)
            attended[here, columns] = jnp.where(
                masks[t * 8 + 7] > 0.5, slot_out, attended[here, columns]
            )
            return carry

        lax.fori_loop(0, heads, body, 0)

    wait_rim((0, 1, 2, 4))
    edge_stages((0, 1, 2))
    lax.fori_loop(0, 3 * heads, first_rim_body, 0)

    load_out_weight.wait()
    load_cached.wait()
    for copies in (to_sibling, to_cross, passed):
        for copy in copies:
            copy.wait_send()
    wait_rim((3, 5, 6, 7))
    edge_stages((3,))

    @pl.when(left_edge + right_edge == 1)
    def _():
        for stage in range(4):
            edge_pass(stage).wait_send()

    pl.semaphore_signal(free_sem, inc=1, device_id=(g, sibling), device_id_type=MESH)
    second_rim_tile(far_tile)
    second_rim_tile(1)
    pl.semaphore_wait(free_sem, 1)

    def partial_sums(first, second):
        both = jnp.concatenate(
            [attended[pl.ds(aligned(first), chunk), :], attended[pl.ds(aligned(second), chunk), :]],
            axis=0,
        )
        return jnp.dot(both, out_weight[...], preferred_element_type=F32).astype(BF16)

    sums = []

    def project_out(slot, step, chip, chunk_at):
        owner = chip * 2 * rows + chunk_at * chunk
        both = partial_sums(owner + c * rows, owner + (1 - c) * rows)
        half = slot // 3
        rows_buffer[pl.ds((3 * half + step) * chunk, chunk), :] = both[:chunk]
        rows_buffer[pl.ds((6 + slot) * chunk, chunk), :] = both[chunk:]
        copy = pltpu.make_async_remote_copy(
            src_ref=rows_buffer.at[pl.ds((6 + slot) * chunk, chunk), :],
            dst_ref=rim_rows.at[pl.ds(slot * chunk, chunk), :],
            send_sem=sums_send.at[slot],
            recv_sem=sums_recv.at[slot],
            device_id=(g, sibling),
            device_id_type=MESH,
        )
        copy.start()
        sums.append(copy)

    last = []

    def send_last(step):
        sums[step].wait_recv()
        here = pl.ds(step * chunk, chunk)
        kept = rows_buffer[here, :].astype(F32)
        rows_buffer[here, :] = (kept + rim_rows[here, :].astype(F32)).astype(BF16)
        copy = pltpu.make_async_remote_copy(
            src_ref=rows_buffer.at[pl.ds(step * chunk, chunk), :],
            dst_ref=cross_sums.at[step],
            send_sem=last_send.at[step],
            recv_sem=last_recv.at[step],
            device_id=(g, cross),
            device_id_type=MESH,
        )
        copy.start()
        last.append(copy)

    for step in range(3):
        project_out(step, step, 1 - y, step)
        if step > 0:
            send_last(step - 1)
    send_last(2)
    second_rim_tile(near_tile)
    for step in range(3):
        project_out(3 + step, step, y, step)
    stores = []
    for step in range(3):
        sums[3 + step].wait_recv()
        last[step].wait_recv()
        here = pl.ds(step * chunk, chunk)
        total = (
            rows_buffer[pl.ds((3 + step) * chunk, chunk), :].astype(F32)
            + rim_rows[pl.ds((3 + step) * chunk, chunk), :].astype(F32)
            + cross_sums[step].astype(F32)
        )
        latents[here, :] = (latents[here, :].astype(F32) + gate_ref[...] * total).astype(BF16)
        store = pltpu.make_async_copy(
            latents.at[here, :], out_hbm.at[here, :], local_sem.at[step]
        )
        store.start()
        stores.append(store)
    for store in stores:
        store.wait()
    for copy in sums + last:
        copy.wait_send()
    for side in range(2):
        for slot in range(8):
            tile_copy(side, slot).wait_send()


def on_device(
    latents,
    mod_shift,
    mod_scale,
    mod_gate,
    packed_weight,
    query_gain,
    key_gain,
    output_weight,
    cached,
    active_tiles,
    active_count,
    window_tiles,
    window_count,
):
    rows, width = latents.shape
    groups, tiles, window = window_tiles.shape
    share = cached.shape[1]
    heads = share // HD
    slab = cached.shape[0]
    tile = slab // tiles
    chunk = tile // 4
    assert width == 4 * share and tiles == 3 and rows == 3 * chunk and slab == 4 * rows
    anywhere = pl.BlockSpec(memory_space=pl.ANY)
    vmem = pl.BlockSpec(memory_space=pltpu.VMEM)
    smem = pl.BlockSpec(memory_space=pltpu.SMEM)
    dma = pltpu.SemaphoreType.DMA
    return pl.pallas_call(
        functools.partial(kernel, (groups, heads, tile, width, window)),
        out_shape=jax.ShapeDtypeStruct((rows, width), BF16),
        in_specs=[
            anywhere,
            vmem,
            vmem,
            vmem,
            anywhere,
            vmem,
            vmem,
            anywhere,
            anywhere,
            smem,
            smem,
            smem,
            smem,
        ],
        out_specs=anywhere,
        scratch_shapes=[
            pltpu.VMEM((rows, width), BF16),
            pltpu.VMEM((slab, width), BF16),
            pltpu.VMEM((width, 3 * share), BF16),
            pltpu.VMEM((slab, share), BF16),
            pltpu.VMEM((slab, 2 * share), BF16),
            pltpu.VMEM((2, 8, chunk, 2 * share), BF16),
            pltpu.VMEM((2, 2, tile, 2 * share), BF16),
            pltpu.VMEM((8 * chunk, width), BF16),
            pltpu.VMEM((slab, share), F32),
            pltpu.VMEM((slab, share), F32),
            pltpu.VMEM((slab, share), BF16),
            pltpu.VMEM((share, width), BF16),
            pltpu.VMEM((3, chunk, width), BF16),
            pltpu.SMEM((24,), F32),
            dma((6,)),
            dma((3,)),
            dma((3,)),
            dma((3,)),
            dma((3,)),
            dma((3,)),
            dma((3,)),
            dma((2, 8)),
            dma((2, 8)),
            dma((4,)),
            dma((4,)),
            dma((6,)),
            dma((6,)),
            dma((3,)),
            dma((3,)),
            pltpu.SemaphoreType.REGULAR,
        ],
        compiler_params=pltpu.CompilerParams(
            collective_id=0, has_side_effects=True, vmem_limit_bytes=VMEM_LIMIT
        ),
    )(
        latents,
        mod_shift[None],
        mod_scale[None],
        mod_gate[None],
        packed_weight,
        query_gain[None],
        key_gain[None],
        output_weight,
        cached,
        active_tiles,
        active_count,
        window_tiles,
        window_count,
    )


VMEM_LIMIT = 64 * 1024 * 1024


def solution(mesh):
    in_specs = (
        P(("frame", "head"), None),
        P(),
        P(),
        P(),
        P(None, "head"),
        P(),
        P(),
        P("head", None),
        P("frame", "head"),
        P("frame", None),
        P("frame"),
        P(),
        P("frame", None),
    )
    return jax.shard_map(
        on_device,
        mesh=mesh,
        in_specs=in_specs,
        out_specs=P(("frame", "head"), None),
        check_vma=False,
    )
```

```python
import functools
import math

import jax
import jax.numpy as jnp
from jax import lax
from jax.experimental import pallas as pl
from jax.experimental.pallas import tpu as pltpu
from jax.sharding import PartitionSpec as P

HD = 128
ROW = 4
BF16 = jnp.bfloat16
F32 = jnp.float32
MESH = pl.DeviceIdType.MESH


def kernel(
    sizes,
    latents_hbm,
    shift_ref,
    scale_ref,
    gate_ref,
    weight_hbm,
    query_gain_ref,
    key_gain_ref,
    out_weight_hbm,
    cached_hbm,
    active_tiles_ref,
    active_count_ref,
    window_tiles_ref,
    window_count_ref,
    out_hbm,
    latents,
    rows_buffer,
    weight,
    queries,
    bank,
    rim_send,
    rim,
    rim_rows,
    numerator,
    totals,
    attended,
    out_weight,
    cross_sums,
    masks,
    local_sem,
    near_sib_send,
    near_sib_recv,
    cross_send,
    cross_recv,
    pass_send,
    pass_recv,
    rim_send_sem,
    rim_recv_sem,
    rim_pass_send,
    rim_pass_recv,
    sums_send,
    sums_recv,
    last_send,
    last_recv,
    free_sem,
):
    groups, heads, tile, width, window = sizes
    share = heads * HD
    chunk = tile // 4
    rows = 3 * chunk
    g = lax.axis_index("frame")
    h = lax.axis_index("head")
    y = h // 2
    c = h % 2
    sibling = y * 2 + (1 - c)
    cross = (1 - y) * 2 + c
    right = (g + 1) % groups
    left = (g + groups - 1) % groups
    left_edge = (ROW - g % ROW) // ROW
    right_edge = (g % ROW + 1) // ROW
    left_partner = (left, h + left_edge * (cross - h))
    right_partner = (right, h + right_edge * (cross - h))
    edge_side = right_edge

    def aligned(start):
        return pl.multiple_of(start, chunk)

    def far_place(step, core):
        return aligned((6 + 2 * step + core) * chunk)

    load_latents = pltpu.make_async_copy(latents_hbm, latents, local_sem.at[0])
    load_latents.start()
    parts = 3
    part_width = 3 * share // parts
    load_weight = [
        pltpu.make_async_copy(
            weight_hbm.at[:, pl.ds(part * part_width, part_width)],
            weight.at[:, pl.ds(part * part_width, part_width)],
            local_sem.at[1 + part],
        )
        for part in range(parts)
    ]
    for load in load_weight:
        load.start()
    load_out_weight = pltpu.make_async_copy(out_weight_hbm, out_weight, local_sem.at[4])
    load_cached = pltpu.make_async_copy(cached_hbm, attended, local_sem.at[5])

    barrier = pltpu.get_barrier_semaphore()
    for partner in ((g, sibling), (g, cross), left_partner, right_partner):
        pl.semaphore_signal(barrier, inc=1, device_id=partner, device_id_type=MESH)
    pl.semaphore_wait(barrier, 4)

    load_latents.wait()
    to_sibling, to_cross = [], []
    for step in range(3):
        mine = (1 - y) * (2 - step) + y * step
        x = latents[pl.ds(aligned(mine * chunk), chunk), :].astype(F32)
        centred = x - jnp.mean(x, axis=-1, keepdims=True)
        variance = jnp.mean(centred * centred, axis=-1, keepdims=True)
        normed = (
            centred * lax.rsqrt(variance + 1e-06) * (1.0 + scale_ref[...]) + shift_ref[...]
        ).astype(BF16)
        place = aligned(c * rows + mine * chunk)
        rows_buffer[pl.ds(place, chunk), :] = normed
        over = pltpu.make_async_remote_copy(
            src_ref=rows_buffer.at[pl.ds(place, chunk), :],
            dst_ref=rows_buffer.at[pl.ds(far_place(step, c), chunk), :],
            send_sem=cross_send.at[step],
            recv_sem=cross_recv.at[step],
            device_id=(g, cross),
            device_id_type=MESH,
        )
        over.start()
        to_cross.append(over)
        beside = pltpu.make_async_remote_copy(
            src_ref=rows_buffer.at[pl.ds(place, chunk), :],
            dst_ref=rows_buffer.at[pl.ds(place, chunk), :],
            send_sem=near_sib_send.at[step],
            recv_sem=near_sib_recv.at[step],
            device_id=(g, sibling),
            device_id_type=MESH,
        )
        beside.start()
        to_sibling.append(beside)

    def rim_tiles(reader, owner):
        used = [jnp.int32(0)] * 3
        for j in range(3):
            for w in range(window):
                entry = window_tiles_ref[reader, j, w]
                for t in range(3):
                    used[t] = used[t] | (entry == owner * 3 + t).astype(jnp.int32)
        spare = jnp.where(used[1] == 0, 1, jnp.where(used[0] == 0, 0, 2))
        return jnp.where(spare == 0, 1, 0), jnp.where(spare == 2, 1, 2)

    send_tiles = [rim_tiles(right, g), rim_tiles(left, g)]
    recv_tiles = [rim_tiles(g, left), rim_tiles(g, right)]
    candidates = [g * 3, g * 3 + 1, g * 3 + 2]
    for side, owner in ((0, left), (1, right)):
        candidates += [owner * 3 + recv_tiles[side][0], owner * 3 + recv_tiles[side][1]]
    named = []
    for j in range(3):
        hits = [jnp.int32(0)] * 7
        for w in range(window):
            entry = window_tiles_ref[g, j, w]
            inside = (w < window_count_ref[0, j]).astype(jnp.int32)
            for k in range(7):
                hits[k] = hits[k] + inside * (entry == candidates[k]).astype(jnp.int32)
        named.append(hits)
    for t in range(3):
        holds = [
            ((active_tiles_ref[0, j] == t) & (j < active_count_ref[0])).astype(jnp.int32)
            for j in range(3)
        ]
        for k in range(7):
            masks[t * 8 + k] = sum(holds[j] * named[j][k] for j in range(3)).astype(F32)
        masks[t * 8 + 7] = sum(holds).astype(F32)

    def head_norm(vectors, gain_ref):
        mean_square = jnp.mean(vectors * vectors, axis=-1, keepdims=True)
        return (vectors * lax.rsqrt(mean_square + 1e-06) * gain_ref[...]).astype(BF16)

    pair = 2 * 3 * HD

    def project(block_at, places):
        def body(step, carry):
            columns = pl.ds(pl.multiple_of(step * pair, pair), pair)
            packed = jnp.dot(rows_buffer[block_at, :], weight[:, columns], preferred_element_type=F32)
            for half in range(2):
                at = half * 3 * HD
                head = step * 2 + half
                query_columns = pl.ds(pl.multiple_of(head * HD, HD), HD)
                value_columns = pl.ds(pl.multiple_of(share + head * HD, HD), HD)
                q = head_norm(packed[:, at : at + HD], query_gain_ref)
                k = head_norm(packed[:, at + HD : at + 2 * HD], key_gain_ref)
                v = packed[:, at + 2 * HD : at + 3 * HD].astype(BF16)
                for first, place, count in places:
                    queries[pl.ds(place, count), query_columns] = q[first : first + count]
                    bank[pl.ds(place, count), query_columns] = k[first : first + count]
                    bank[pl.ds(place, count), value_columns] = v[first : first + count]
            return carry

        lax.fori_loop(0, heads // 2, body, 0)

    order = ((0, 0), (0, 1), (0, 2), (1, 1), (0, 3), (1, 2), (1, 0), (1, 3))

    def quarter_of(slot, chip):
        second, quarter = order[slot]
        return second + chip * (1 - 2 * second), quarter + chip * (3 - 2 * quarter)

    def row_place(piece):
        chip, inside = piece // 6, piece % 6
        away = (chip + y) % 2
        number = inside % 3
        step = y * (2 - number) + (1 - y) * number
        return aligned(
            (1 - away) * inside * chunk + away * (6 + 2 * step + inside // 3) * chunk
        )

    half_width = width // 2

    def tile_copy(side, slot):
        second, quarter = quarter_of(slot, y)
        return pltpu.make_async_remote_copy(
            src_ref=rim_send.at[side, slot],
            dst_ref=rim.at[side, second, pl.ds(aligned(quarter * chunk), chunk), :],
            send_sem=rim_send_sem.at[side, slot],
            recv_sem=rim_recv_sem.at[side, slot],
            device_id=(right if side == 0 else left, h),
            device_id_type=MESH,
        )

    def edge_copy(side, slot):
        stage, half = slot // 2, slot % 2
        target = left + (1 - side) * (right - left)
        return pltpu.make_async_remote_copy(
            src_ref=rim_send.at[side, slot],
            dst_ref=rim_rows.at[
                pl.ds(aligned((2 * stage + c) * chunk), chunk),
                pl.ds(half * half_width, half_width),
            ],
            send_sem=rim_send_sem.at[side, slot],
            recv_sem=rim_recv_sem.at[side, slot],
            device_id=(target, cross),
            device_id_type=MESH,
        )

    def edge_pass(stage):
        here = pl.ds(aligned((2 * stage + c) * chunk), chunk)
        return pltpu.make_async_remote_copy(
            src_ref=rim_rows.at[here, :],
            dst_ref=rim_rows.at[here, :],
            send_sem=rim_pass_send.at[stage],
            recv_sem=rim_pass_recv.at[stage],
            device_id=(g, sibling),
            device_id_type=MESH,
        )

    def takes_high(side, second):
        first_tile, second_tile = send_tiles[side]
        return jnp.where(second == 0, first_tile, second_tile - 1) == 1

    def send_tiles_of(stage):
        for side in range(2):
            edge = right_edge if side == 0 else left_edge

            @pl.when(edge == 0)
            def _():
                for slot in (2 * stage, 2 * stage + 1):
                    second, quarter = quarter_of(slot, y)
                    low = bank[pl.ds(aligned((4 * second + quarter) * chunk), chunk), :]
                    high = bank[pl.ds(aligned((4 * second + quarter + 4) * chunk), chunk), :]
                    rim_send[side, slot] = jnp.where(takes_high(side, second), high, low)
                    tile_copy(side, slot).start()

    def send_rows_of(stage):
        for side in range(2):
            edge = right_edge if side == 0 else left_edge

            @pl.when(edge == 1)
            def _():
                second, quarter = (
                    (1 - c) * even + c * odd
                    for even, odd in zip(quarter_of(2 * stage, y), quarter_of(2 * stage + 1, y))
                )
                low = row_place(4 * second + quarter)
                high = row_place(4 * second + quarter + 4)
                for half in range(2):
                    columns = pl.ds(half * half_width, half_width)
                    rim_send[side, 2 * stage + half] = jnp.where(
                        takes_high(side, second),
                        rows_buffer[pl.ds(high, chunk), columns],
                        rows_buffer[pl.ds(low, chunk), columns],
                    )
                    edge_copy(side, 2 * stage + half).start()

    def wait_rim(slots):
        for side in range(2):
            edge = left_edge if side == 0 else right_edge

            @pl.when(edge == 0)
            def _():
                for slot in slots:
                    tile_copy(side, slot).wait_recv()

    def pass_edge(stage):
        @pl.when(left_edge + right_edge == 1)
        def _():
            for half in range(2):
                edge_copy(edge_side, 2 * stage + half).wait_recv()
            edge_pass(stage).start()

    def project_edge(stage):
        @pl.when(left_edge + right_edge == 1)
        def _():
            edge_pass(stage).wait_recv()
            places = []
            for core in range(2):
                second, quarter = quarter_of(2 * stage + core, 1 - y)
                places.append((core * chunk, second, aligned(quarter * chunk)))

            def body(step, carry):
                for head in (2 * step, 2 * step + 1):
                    columns = pl.ds(pl.multiple_of(head * 3 * HD + HD, HD), 2 * HD)
                    packed = jnp.dot(
                        rim_rows[pl.ds(2 * stage * chunk, 2 * chunk), :],
                        weight[:, columns],
                        preferred_element_type=F32,
                    )
                    k = head_norm(packed[:, :HD], key_gain_ref)
                    v = packed[:, HD:].astype(BF16)
                    key_columns = pl.ds(pl.multiple_of(head * HD, HD), HD)
                    value_columns = pl.ds(pl.multiple_of(share + head * HD, HD), HD)
                    for first, second, place in places:
                        there = pl.ds(place, chunk)
                        rim[edge_side, second, there, key_columns] = k[first : first + chunk]
                        rim[edge_side, second, there, value_columns] = v[first : first + chunk]
                return carry

            lax.fori_loop(0, heads // 2, body, 0)

    log_scale = math.log2(math.e) / math.sqrt(HD)
    near_tile = y * 2
    far_tile = (1 - y) * 2

    def attend(q, keys, values, names):
        scores = lax.dot_general(q, keys, (((1,), (1,)), ((), ())), preferred_element_type=F32)
        weights = jnp.exp2(scores * log_scale)
        weights = jnp.concatenate(
            [weights[:, k * tile : (k + 1) * tile] * name for k, name in enumerate(names)], axis=1
        )
        total = weights[:, :HD]
        for at in range(HD, weights.shape[1], HD):
            total = total + weights[:, at : at + HD]
        return jnp.dot(weights.astype(BF16), values, preferred_element_type=F32), total

    def columns_of(head):
        return (
            pl.ds(pl.multiple_of(head * HD, HD), HD),
            pl.ds(pl.multiple_of(share + head * HD, HD), HD),
        )

    def over_heads(work, unroll):
        def body(step, carry):
            for inner in range(unroll):
                work(step * unroll + inner)
            return carry

        lax.fori_loop(0, heads // unroll, body, 0)

    def own_pairs(t, first_key, count, fresh, head):
        here = pl.ds(aligned(t * tile), tile)
        there = pl.ds(aligned(first_key * tile), count * tile)
        columns, value_columns = columns_of(head)
        out, total = attend(
            queries[here, columns],
            bank[there, columns],
            bank[there, value_columns],
            [masks[t * 8 + first_key + k] for k in range(count)],
        )
        if not fresh:
            out, total = numerator[here, columns] + out, totals[here, columns] + total
        numerator[here, columns] = out
        totals[here, columns] = total

    def rim_pairs(t, phase, head):
        here = pl.ds(aligned(t * tile), tile)
        columns, value_columns = columns_of(head)
        keys, values, names = [], [], []
        for side in range(2):
            edge = left_edge if side == 0 else right_edge
            second = (y + edge + phase) % 2
            keys.append(rim[side, second, :, columns])
            values.append(rim[side, second, :, value_columns])
            names.append(masks[t * 8 + 3 + 2 * side + second])
        out, total = attend(
            queries[here, columns],
            jnp.concatenate(keys, axis=0),
            jnp.concatenate(values, axis=0),
            names,
        )
        out, total = numerator[here, columns] + out, totals[here, columns] + total
        if phase == 0:
            numerator[here, columns] = out
            totals[here, columns] = total
        else:
            slot_out = (out / jnp.sum(total, axis=-1, keepdims=True)).astype(BF16)
            attended[here, columns] = jnp.where(
                masks[t * 8 + 7] > 0.5, slot_out, attended[here, columns]
            )

    half_heads = heads // 2

    for load in load_weight:
        load.wait()
    load_out_weight.start()
    load_cached.start()
    for copy in to_sibling:
        copy.wait_recv()
    send_rows_of(0)
    project(pl.ds(0, 2 * rows), [(0, aligned(y * 2 * rows), 2 * rows)])
    send_tiles_of(0)
    passed = []
    for step in range(3):
        to_cross[step].wait_recv()
        onward = pltpu.make_async_remote_copy(
            src_ref=rows_buffer.at[pl.ds(far_place(step, c), chunk), :],
            dst_ref=rows_buffer.at[pl.ds(far_place(step, c), chunk), :],
            send_sem=pass_send.at[step],
            recv_sem=pass_recv.at[step],
            device_id=(g, sibling),
            device_id_type=MESH,
        )
        onward.start()
        passed.append(onward)
        onward.wait_recv()
        send_rows_of(step + 1)
        if step > 0:
            pass_edge(step - 1)
        theirs = y * (2 - step) + (1 - y) * step
        start = (1 - y) * 2 * rows + theirs * chunk
        project(
            pl.ds(far_place(step, 0), 2 * chunk),
            [(0, aligned(start), chunk), (chunk, aligned(start + rows), chunk)],
        )
        send_tiles_of(step + 1)
        if step == 0:
            over_heads(lambda head: own_pairs(near_tile, near_tile, 1, True, head), half_heads)
        if step == 1:

            def two_tiles(head):
                own_pairs(near_tile, 1, 1, False, head)
                own_pairs(1, y, 2, True, head)

            over_heads(two_tiles, 1)
            project_edge(0)
    project_edge(1)
    pass_edge(2)

    def three_tiles(head):
        own_pairs(near_tile, far_tile, 1, False, head)
        own_pairs(1, far_tile, 1, False, head)
        own_pairs(far_tile, 0, 3, True, head)

    over_heads(three_tiles, 1)
    project_edge(2)
    pass_edge(3)
    wait_rim((0, 1, 2, 4))

    def first_rim(head):
        for t in range(3):
            rim_pairs(t, 0, head)

    over_heads(first_rim, 1)
    load_out_weight.wait()
    load_cached.wait()
    for copies in (to_sibling, to_cross, passed):
        for copy in copies:
            copy.wait_send()
    wait_rim((3, 5, 6, 7))
    project_edge(3)

    @pl.when(left_edge + right_edge == 1)
    def _():
        for stage in range(4):
            edge_pass(stage).wait_send()

    pl.semaphore_signal(free_sem, inc=1, device_id=(g, sibling), device_id_type=MESH)
    over_heads(lambda head: rim_pairs(far_tile, 1, head), half_heads)
    pl.semaphore_wait(free_sem, 1)

    def partial_sums(first, second):
        both = jnp.concatenate(
            [attended[pl.ds(aligned(first), chunk), :], attended[pl.ds(aligned(second), chunk), :]],
            axis=0,
        )
        return jnp.dot(both, out_weight[...], preferred_element_type=F32).astype(BF16)

    sums = []

    def project_out(slot, step, chip, chunk_at):
        owner = chip * 2 * rows + chunk_at * chunk
        both = partial_sums(owner + c * rows, owner + (1 - c) * rows)
        half = slot // 3
        rows_buffer[pl.ds((3 * half + step) * chunk, chunk), :] = both[:chunk]
        rows_buffer[pl.ds((6 + slot) * chunk, chunk), :] = both[chunk:]
        copy = pltpu.make_async_remote_copy(
            src_ref=rows_buffer.at[pl.ds((6 + slot) * chunk, chunk), :],
            dst_ref=rim_rows.at[pl.ds(slot * chunk, chunk), :],
            send_sem=sums_send.at[slot],
            recv_sem=sums_recv.at[slot],
            device_id=(g, sibling),
            device_id_type=MESH,
        )
        copy.start()
        sums.append(copy)

    last = []

    def send_last(step):
        sums[step].wait_recv()
        here = pl.ds(step * chunk, chunk)
        kept = rows_buffer[here, :].astype(F32)
        rows_buffer[here, :] = (kept + rim_rows[here, :].astype(F32)).astype(BF16)
        copy = pltpu.make_async_remote_copy(
            src_ref=rows_buffer.at[pl.ds(step * chunk, chunk), :],
            dst_ref=cross_sums.at[step],
            send_sem=last_send.at[step],
            recv_sem=last_recv.at[step],
            device_id=(g, cross),
            device_id_type=MESH,
        )
        copy.start()
        last.append(copy)

    for step in range(3):
        project_out(step, step, 1 - y, (1 - y) * (2 - step) + y * step)
        if step == 0:
            over_heads(lambda head: rim_pairs(1, 1, head), half_heads)
        send_last(step)
    over_heads(lambda head: rim_pairs(near_tile, 1, head), half_heads)
    for step in range(3):
        project_out(3 + step, step, y, y * (2 - step) + (1 - y) * step)
    stores = []
    for step in range(3):
        sums[3 + step].wait_recv()
        last[step].wait_recv()
        here = pl.ds(aligned((y * (2 - step) + (1 - y) * step) * chunk), chunk)
        total = (
            rows_buffer[pl.ds((3 + step) * chunk, chunk), :].astype(F32)
            + rim_rows[pl.ds((3 + step) * chunk, chunk), :].astype(F32)
            + cross_sums[step].astype(F32)
        )
        latents[here, :] = (latents[here, :].astype(F32) + gate_ref[...] * total).astype(BF16)
        store = pltpu.make_async_copy(
            latents.at[here, :], out_hbm.at[here, :], local_sem.at[step]
        )
        store.start()
        stores.append(store)
    for store in stores:
        store.wait()
    for copy in sums + last:
        copy.wait_send()
    for side in range(2):
        for slot in range(8):
            tile_copy(side, slot).wait_send()


def on_device(
    latents,
    mod_shift,
    mod_scale,
    mod_gate,
    packed_weight,
    query_gain,
    key_gain,
    output_weight,
    cached,
    active_tiles,
    active_count,
    window_tiles,
    window_count,
):
    rows, width = latents.shape
    groups, tiles, window = window_tiles.shape
    share = cached.shape[1]
    heads = share // HD
    slab = cached.shape[0]
    tile = slab // tiles
    chunk = tile // 4
    assert width == 4 * share and tiles == 3 and rows == 3 * chunk and slab == 4 * rows
    anywhere = pl.BlockSpec(memory_space=pl.ANY)
    vmem = pl.BlockSpec(memory_space=pltpu.VMEM)
    smem = pl.BlockSpec(memory_space=pltpu.SMEM)
    dma = pltpu.SemaphoreType.DMA
    return pl.pallas_call(
        functools.partial(kernel, (groups, heads, tile, width, window)),
        out_shape=jax.ShapeDtypeStruct((rows, width), BF16),
        in_specs=[
            anywhere,
            vmem,
            vmem,
            vmem,
            anywhere,
            vmem,
            vmem,
            anywhere,
            anywhere,
            smem,
            smem,
            smem,
            smem,
        ],
        out_specs=anywhere,
        scratch_shapes=[
            pltpu.VMEM((rows, width), BF16),
            pltpu.VMEM((slab, width), BF16),
            pltpu.VMEM((width, 3 * share), BF16),
            pltpu.VMEM((slab, share), BF16),
            pltpu.VMEM((slab, 2 * share), BF16),
            pltpu.VMEM((2, 8, chunk, 2 * share), BF16),
            pltpu.VMEM((2, 2, tile, 2 * share), BF16),
            pltpu.VMEM((8 * chunk, width), BF16),
            pltpu.VMEM((slab, share), F32),
            pltpu.VMEM((slab, share), F32),
            pltpu.VMEM((slab, share), BF16),
            pltpu.VMEM((share, width), BF16),
            pltpu.VMEM((3, chunk, width), BF16),
            pltpu.SMEM((24,), F32),
            dma((6,)),
            dma((3,)),
            dma((3,)),
            dma((3,)),
            dma((3,)),
            dma((3,)),
            dma((3,)),
            dma((2, 8)),
            dma((2, 8)),
            dma((4,)),
            dma((4,)),
            dma((6,)),
            dma((6,)),
            dma((3,)),
            dma((3,)),
            pltpu.SemaphoreType.REGULAR,
        ],
        compiler_params=pltpu.CompilerParams(
            collective_id=0, has_side_effects=True, vmem_limit_bytes=VMEM_LIMIT
        ),
    )(
        latents,
        mod_shift[None],
        mod_scale[None],
        mod_gate[None],
        packed_weight,
        query_gain[None],
        key_gain[None],
        output_weight,
        cached,
        active_tiles,
        active_count,
        window_tiles,
        window_count,
    )


VMEM_LIMIT = 64 * 1024 * 1024


def solution(mesh):
    in_specs = (
        P(("frame", "head"), None),
        P(),
        P(),
        P(),
        P(None, "head"),
        P(),
        P(),
        P("head", None),
        P("frame", "head"),
        P("frame", None),
        P("frame"),
        P(),
        P("frame", None),
    )
    return jax.shard_map(
        on_device,
        mesh=mesh,
        in_specs=in_specs,
        out_specs=P(("frame", "head"), None),
        check_vma=False,
    )
```

```python
import functools
import math

import jax
import jax.numpy as jnp
from jax import lax
from jax.experimental import pallas as pl
from jax.experimental.pallas import tpu as pltpu
from jax.sharding import PartitionSpec as P

HD = 128
ROW = 4
BF16 = jnp.bfloat16
F32 = jnp.float32
MESH = pl.DeviceIdType.MESH


def kernel(
    sizes,
    latents_hbm,
    shift_ref,
    scale_ref,
    gate_ref,
    weight_hbm,
    query_gain_ref,
    key_gain_ref,
    out_weight_hbm,
    cached_hbm,
    active_tiles_ref,
    active_count_ref,
    window_tiles_ref,
    window_count_ref,
    out_hbm,
    latents,
    rows_buffer,
    weight,
    queries,
    bank,
    rim_send,
    rim,
    rim_rows,
    numerator,
    totals,
    attended,
    out_weight,
    cross_sums,
    masks,
    local_sem,
    near_sib_send,
    near_sib_recv,
    cross_send,
    cross_recv,
    pass_send,
    pass_recv,
    rim_send_sem,
    rim_recv_sem,
    rim_pass_send,
    rim_pass_recv,
    sums_send,
    sums_recv,
    last_send,
    last_recv,
    free_sem,
):
    groups, heads, tile, width, window = sizes
    share = heads * HD
    chunk = tile // 4
    rows = 3 * chunk
    g = lax.axis_index("frame")
    h = lax.axis_index("head")
    y = h // 2
    c = h % 2
    sibling = y * 2 + (1 - c)
    cross = (1 - y) * 2 + c
    right = (g + 1) % groups
    left = (g + groups - 1) % groups
    left_edge = (ROW - g % ROW) // ROW
    right_edge = (g % ROW + 1) // ROW
    left_partner = (left, h + left_edge * (cross - h))
    right_partner = (right, h + right_edge * (cross - h))
    edge_side = right_edge
    first_group = (groups - g) // groups
    last_group = (g + 1) // groups
    edge_here = left_edge - first_group + right_edge - last_group

    def aligned(start):
        return pl.multiple_of(start, chunk)

    def far_place(step, core):
        return aligned((6 + 2 * step + core) * chunk)

    load_latents = pltpu.make_async_copy(latents_hbm, latents, local_sem.at[0])
    load_latents.start()
    parts = 3
    part_width = 3 * share // parts
    load_weight = [
        pltpu.make_async_copy(
            weight_hbm.at[:, pl.ds(part * part_width, part_width)],
            weight.at[:, pl.ds(part * part_width, part_width)],
            local_sem.at[1 + part],
        )
        for part in range(parts)
    ]
    for load in load_weight:
        load.start()
    load_out_weight = pltpu.make_async_copy(out_weight_hbm, out_weight, local_sem.at[4])
    load_cached = pltpu.make_async_copy(cached_hbm, attended, local_sem.at[5])

    barrier = pltpu.get_barrier_semaphore()
    for partner, absent in (
        ((g, sibling), 0),
        ((g, cross), 0),
        (left_partner, first_group),
        (right_partner, last_group),
    ):

        @pl.when(absent == 0)
        def _():
            pl.semaphore_signal(barrier, inc=1, device_id=partner, device_id_type=MESH)

    pl.semaphore_wait(barrier, 4 - first_group - last_group)

    load_latents.wait()
    to_sibling, to_cross = [], []
    for step in range(3):
        mine = (1 - y) * (2 - step) + y * step
        x = latents[pl.ds(aligned(mine * chunk), chunk), :].astype(F32)
        centred = x - jnp.mean(x, axis=-1, keepdims=True)
        variance = jnp.mean(centred * centred, axis=-1, keepdims=True)
        normed = (
            centred * lax.rsqrt(variance + 1e-06) * (1.0 + scale_ref[...]) + shift_ref[...]
        ).astype(BF16)
        place = aligned(c * rows + mine * chunk)
        rows_buffer[pl.ds(place, chunk), :] = normed
        over = pltpu.make_async_remote_copy(
            src_ref=rows_buffer.at[pl.ds(place, chunk), :],
            dst_ref=rows_buffer.at[pl.ds(far_place(step, c), chunk), :],
            send_sem=cross_send.at[step],
            recv_sem=cross_recv.at[step],
            device_id=(g, cross),
            device_id_type=MESH,
        )
        over.start()
        to_cross.append(over)
        beside = pltpu.make_async_remote_copy(
            src_ref=rows_buffer.at[pl.ds(place, chunk), :],
            dst_ref=rows_buffer.at[pl.ds(place, chunk), :],
            send_sem=near_sib_send.at[step],
            recv_sem=near_sib_recv.at[step],
            device_id=(g, sibling),
            device_id_type=MESH,
        )
        beside.start()
        to_sibling.append(beside)

    def rim_tiles(reader, owner):
        used = [jnp.int32(0)] * 3
        for j in range(3):
            for w in range(window):
                entry = window_tiles_ref[w, j, reader]
                for t in range(3):
                    used[t] = used[t] | (entry == owner * 3 + t).astype(jnp.int32)
        spare = jnp.where(used[1] == 0, 1, jnp.where(used[0] == 0, 0, 2))
        return jnp.where(spare == 0, 1, 0), jnp.where(spare == 2, 1, 2)

    send_tiles = [rim_tiles(right, g), rim_tiles(left, g)]
    recv_tiles = [rim_tiles(g, left), rim_tiles(g, right)]
    candidates = [g * 3, g * 3 + 1, g * 3 + 2]
    for side, owner in ((0, left), (1, right)):
        candidates += [owner * 3 + recv_tiles[side][0], owner * 3 + recv_tiles[side][1]]
    named = []
    for j in range(3):
        hits = [jnp.int32(0)] * 7
        for w in range(window):
            entry = window_tiles_ref[w, j, g]
            inside = (w < window_count_ref[0, j]).astype(jnp.int32)
            for k in range(7):
                hits[k] = hits[k] + inside * (entry == candidates[k]).astype(jnp.int32)
        named.append(hits)
    for t in range(3):
        holds = [
            ((active_tiles_ref[0, j] == t) & (j < active_count_ref[0])).astype(jnp.int32)
            for j in range(3)
        ]
        for k in range(7):
            masks[t * 8 + k] = sum(holds[j] * named[j][k] for j in range(3)).astype(F32)
        masks[t * 8 + 7] = sum(holds).astype(F32)

    def head_norm(vectors, gain_ref):
        mean_square = jnp.mean(vectors * vectors, axis=-1, keepdims=True)
        return (vectors * lax.rsqrt(mean_square + 1e-06) * gain_ref[...]).astype(BF16)

    pair = 2 * 3 * HD

    def project(block_at, places):
        def body(step, carry):
            columns = pl.ds(pl.multiple_of(step * pair, pair), pair)
            packed = jnp.dot(rows_buffer[block_at, :], weight[:, columns], preferred_element_type=F32)
            for half in range(2):
                at = half * 3 * HD
                head = step * 2 + half
                query_columns = pl.ds(pl.multiple_of(head * HD, HD), HD)
                value_columns = pl.ds(pl.multiple_of(share + head * HD, HD), HD)
                q = head_norm(packed[:, at : at + HD], query_gain_ref)
                k = head_norm(packed[:, at + HD : at + 2 * HD], key_gain_ref)
                v = packed[:, at + 2 * HD : at + 3 * HD].astype(BF16)
                for first, place, count in places:
                    queries[pl.ds(place, count), query_columns] = q[first : first + count]
                    bank[pl.ds(place, count), query_columns] = k[first : first + count]
                    bank[pl.ds(place, count), value_columns] = v[first : first + count]
            return carry

        lax.fori_loop(0, heads // 2, body, 0)

    order = ((0, 0), (0, 1), (0, 2), (1, 1), (0, 3), (1, 2), (1, 0), (1, 3))

    def quarter_of(slot, chip):
        second, quarter = order[slot]
        return second + chip * (1 - 2 * second), quarter + chip * (3 - 2 * quarter)

    def row_place(piece):
        chip, inside = piece // 6, piece % 6
        away = (chip + y) % 2
        number = inside % 3
        step = y * (2 - number) + (1 - y) * number
        return aligned(
            (1 - away) * inside * chunk + away * (6 + 2 * step + inside // 3) * chunk
        )

    half_width = width // 2

    def tile_copy(side, slot):
        second, quarter = quarter_of(slot, y)
        return pltpu.make_async_remote_copy(
            src_ref=rim_send.at[side, slot],
            dst_ref=rim.at[side, second, pl.ds(aligned(quarter * chunk), chunk), :],
            send_sem=rim_send_sem.at[side, slot],
            recv_sem=rim_recv_sem.at[side, slot],
            device_id=(right if side == 0 else left, h),
            device_id_type=MESH,
        )

    def edge_copy(side, slot):
        stage, half = slot // 2, slot % 2
        target = left + (1 - side) * (right - left)
        return pltpu.make_async_remote_copy(
            src_ref=rim_send.at[side, slot],
            dst_ref=rim_rows.at[
                pl.ds(aligned((2 * stage + c) * chunk), chunk),
                pl.ds(half * half_width, half_width),
            ],
            send_sem=rim_send_sem.at[side, slot],
            recv_sem=rim_recv_sem.at[side, slot],
            device_id=(target, cross),
            device_id_type=MESH,
        )

    def edge_pass(stage):
        here = pl.ds(aligned((2 * stage + c) * chunk), chunk)
        return pltpu.make_async_remote_copy(
            src_ref=rim_rows.at[here, :],
            dst_ref=rim_rows.at[here, :],
            send_sem=rim_pass_send.at[stage],
            recv_sem=rim_pass_recv.at[stage],
            device_id=(g, sibling),
            device_id_type=MESH,
        )

    def takes_high(side, second):
        first_tile, second_tile = send_tiles[side]
        return jnp.where(second == 0, first_tile, second_tile - 1) == 1

    def send_tiles_of(stage):
        for side in range(2):
            edge = right_edge if side == 0 else left_edge

            @pl.when(edge == 0)
            def _():
                for slot in (2 * stage, 2 * stage + 1):
                    second, quarter = quarter_of(slot, y)
                    low = bank[pl.ds(aligned((4 * second + quarter) * chunk), chunk), :]
                    high = bank[pl.ds(aligned((4 * second + quarter + 4) * chunk), chunk), :]
                    rim_send[side, slot] = jnp.where(takes_high(side, second), high, low)
                    tile_copy(side, slot).start()

    def send_rows_of(stage):
        for side in range(2):
            edge = right_edge if side == 0 else left_edge

            @pl.when(edge - (last_group if side == 0 else first_group) == 1)
            def _():
                second, quarter = (
                    (1 - c) * even + c * odd
                    for even, odd in zip(quarter_of(2 * stage, y), quarter_of(2 * stage + 1, y))
                )
                low = row_place(4 * second + quarter)
                high = row_place(4 * second + quarter + 4)
                for half in range(2):
                    columns = pl.ds(half * half_width, half_width)
                    rim_send[side, 2 * stage + half] = jnp.where(
                        takes_high(side, second),
                        rows_buffer[pl.ds(high, chunk), columns],
                        rows_buffer[pl.ds(low, chunk), columns],
                    )
                    edge_copy(side, 2 * stage + half).start()

    def wait_rim(slots):
        for side in range(2):
            edge = left_edge if side == 0 else right_edge

            @pl.when(edge == 0)
            def _():
                for slot in slots:
                    tile_copy(side, slot).wait_recv()

    def pass_edge(stage):
        @pl.when(edge_here == 1)
        def _():
            for half in range(2):
                edge_copy(edge_side, 2 * stage + half).wait_recv()
            edge_pass(stage).start()

    def project_edge(stage):
        @pl.when(edge_here == 1)
        def _():
            edge_pass(stage).wait_recv()
            places = []
            for core in range(2):
                second, quarter = quarter_of(2 * stage + core, 1 - y)
                places.append((core * chunk, second, aligned(quarter * chunk)))

            def body(step, carry):
                for head in (2 * step, 2 * step + 1):
                    columns = pl.ds(pl.multiple_of(head * 3 * HD + HD, HD), 2 * HD)
                    packed = jnp.dot(
                        rim_rows[pl.ds(2 * stage * chunk, 2 * chunk), :],
                        weight[:, columns],
                        preferred_element_type=F32,
                    )
                    k = head_norm(packed[:, :HD], key_gain_ref)
                    v = packed[:, HD:].astype(BF16)
                    key_columns = pl.ds(pl.multiple_of(head * HD, HD), HD)
                    value_columns = pl.ds(pl.multiple_of(share + head * HD, HD), HD)
                    for first, second, place in places:
                        there = pl.ds(place, chunk)
                        rim[edge_side, second, there, key_columns] = k[first : first + chunk]
                        rim[edge_side, second, there, value_columns] = v[first : first + chunk]
                return carry

            lax.fori_loop(0, heads // 2, body, 0)

    log_scale = math.log2(math.e) / math.sqrt(HD)
    near_tile = y * 2
    far_tile = (1 - y) * 2

    def attend(q, keys, values, names):
        scores = lax.dot_general(q, keys, (((1,), (1,)), ((), ())), preferred_element_type=F32)
        weights = jnp.exp2(scores * log_scale)
        weights = jnp.concatenate(
            [weights[:, k * tile : (k + 1) * tile] * name for k, name in enumerate(names)], axis=1
        )
        total = weights[:, :HD]
        for at in range(HD, weights.shape[1], HD):
            total = total + weights[:, at : at + HD]
        return jnp.dot(weights.astype(BF16), values, preferred_element_type=F32), total

    def columns_of(head):
        return (
            pl.ds(pl.multiple_of(head * HD, HD), HD),
            pl.ds(pl.multiple_of(share + head * HD, HD), HD),
        )

    def over_heads(work, unroll):
        def body(step, carry):
            for inner in range(unroll):
                work(step * unroll + inner)
            return carry

        lax.fori_loop(0, heads // unroll, body, 0)

    def own_pairs(t, first_key, count, fresh, head):
        here = pl.ds(aligned(t * tile), tile)
        there = pl.ds(aligned(first_key * tile), count * tile)
        columns, value_columns = columns_of(head)
        out, total = attend(
            queries[here, columns],
            bank[there, columns],
            bank[there, value_columns],
            [masks[t * 8 + first_key + k] for k in range(count)],
        )
        if not fresh:
            out, total = numerator[here, columns] + out, totals[here, columns] + total
        numerator[here, columns] = out
        totals[here, columns] = total

    def rim_pairs(t, phases, head):
        here = pl.ds(aligned(t * tile), tile)
        columns, value_columns = columns_of(head)
        keys, values, names = [], [], []
        for phase in phases:
            for side in range(2):
                edge = left_edge if side == 0 else right_edge
                second = (y + edge + phase) % 2
                keys.append(rim[side, second, :, columns])
                values.append(rim[side, second, :, value_columns])
                names.append(masks[t * 8 + 3 + 2 * side + second])
        out, total = attend(
            queries[here, columns],
            jnp.concatenate(keys, axis=0),
            jnp.concatenate(values, axis=0),
            names,
        )
        out, total = numerator[here, columns] + out, totals[here, columns] + total
        if 1 not in phases:
            numerator[here, columns] = out
            totals[here, columns] = total
        else:
            slot_out = (out / jnp.sum(total, axis=-1, keepdims=True)).astype(BF16)
            attended[here, columns] = jnp.where(
                masks[t * 8 + 7] > 0.5, slot_out, attended[here, columns]
            )

    triple = math.gcd(heads, 3)

    @pl.when(first_group + last_group == 1)
    def _():
        rim[edge_side] = jnp.zeros(rim.shape[1:], BF16)

    for load in load_weight:
        load.wait()
    load_out_weight.start()
    load_cached.start()
    for copy in to_sibling:
        copy.wait_recv()
    send_rows_of(0)
    project(pl.ds(0, 2 * rows), [(0, aligned(y * 2 * rows), 2 * rows)])
    send_tiles_of(0)
    passed = []
    for step in range(3):
        to_cross[step].wait_recv()
        onward = pltpu.make_async_remote_copy(
            src_ref=rows_buffer.at[pl.ds(far_place(step, c), chunk), :],
            dst_ref=rows_buffer.at[pl.ds(far_place(step, c), chunk), :],
            send_sem=pass_send.at[step],
            recv_sem=pass_recv.at[step],
            device_id=(g, sibling),
            device_id_type=MESH,
        )
        onward.start()
        passed.append(onward)
        onward.wait_recv()
        send_rows_of(step + 1)
        if step > 0:
            pass_edge(step - 1)
        theirs = y * (2 - step) + (1 - y) * step
        start = (1 - y) * 2 * rows + theirs * chunk
        project(
            pl.ds(far_place(step, 0), 2 * chunk),
            [(0, aligned(start), chunk), (chunk, aligned(start + rows), chunk)],
        )
        send_tiles_of(step + 1)
        if step == 0:
            over_heads(lambda head: own_pairs(near_tile, near_tile, 1, True, head), heads)
        if step == 1:

            def two_tiles(head):
                own_pairs(near_tile, 1, 1, False, head)
                own_pairs(1, y, 2, True, head)

            over_heads(two_tiles, 2)
            project_edge(0)
    project_edge(1)
    pass_edge(2)
    over_heads(lambda head: own_pairs(far_tile, 0, 3, True, head), 2)

    def two_singles(head):
        own_pairs(near_tile, far_tile, 1, False, head)
        own_pairs(1, far_tile, 1, False, head)

    over_heads(two_singles, triple)
    project_edge(2)
    pass_edge(3)
    wait_rim((0, 1, 2, 4))
    over_heads(lambda head: rim_pairs(far_tile, (0,), head), heads)
    load_out_weight.wait()
    load_cached.wait()
    for copies in (to_sibling, to_cross, passed):
        for copy in copies:
            copy.wait_send()
    wait_rim((3, 5, 6, 7))
    project_edge(3)

    @pl.when(edge_here == 1)
    def _():
        for stage in range(4):
            edge_pass(stage).wait_send()

    pl.semaphore_signal(free_sem, inc=1, device_id=(g, sibling), device_id_type=MESH)
    over_heads(lambda head: rim_pairs(far_tile, (1,), head), heads)
    pl.semaphore_wait(free_sem, 1)

    def partial_sums(first, second):
        both = jnp.concatenate(
            [attended[pl.ds(aligned(first), chunk), :], attended[pl.ds(aligned(second), chunk), :]],
            axis=0,
        )
        return jnp.dot(both, out_weight[...], preferred_element_type=F32).astype(BF16)

    sums = []

    def project_out(slot, step, chip, chunk_at):
        owner = chip * 2 * rows + chunk_at * chunk
        both = partial_sums(owner + c * rows, owner + (1 - c) * rows)
        half = slot // 3
        rows_buffer[pl.ds((3 * half + step) * chunk, chunk), :] = both[:chunk]
        rows_buffer[pl.ds((6 + slot) * chunk, chunk), :] = both[chunk:]
        copy = pltpu.make_async_remote_copy(
            src_ref=rows_buffer.at[pl.ds((6 + slot) * chunk, chunk), :],
            dst_ref=rim_rows.at[pl.ds(slot * chunk, chunk), :],
            send_sem=sums_send.at[slot],
            recv_sem=sums_recv.at[slot],
            device_id=(g, sibling),
            device_id_type=MESH,
        )
        copy.start()
        sums.append(copy)

    last = []

    def send_last(step):
        sums[step].wait_recv()
        here = pl.ds(step * chunk, chunk)
        kept = rows_buffer[here, :].astype(F32)
        rows_buffer[here, :] = (kept + rim_rows[here, :].astype(F32)).astype(BF16)
        copy = pltpu.make_async_remote_copy(
            src_ref=rows_buffer.at[pl.ds(step * chunk, chunk), :],
            dst_ref=cross_sums.at[step],
            send_sem=last_send.at[step],
            recv_sem=last_recv.at[step],
            device_id=(g, cross),
            device_id_type=MESH,
        )
        copy.start()
        last.append(copy)

    for step in range(3):
        project_out(step, step, 1 - y, (1 - y) * (2 - step) + y * step)
        if step == 0:
            over_heads(lambda head: rim_pairs(1, (0, 1), head), 2)
        send_last(step)
    over_heads(lambda head: rim_pairs(near_tile, (0, 1), head), 2)
    for step in range(3):
        project_out(3 + step, step, y, y * (2 - step) + (1 - y) * step)
    stores = []
    for step in range(3):
        sums[3 + step].wait_recv()
        last[step].wait_recv()
        here = pl.ds(aligned((y * (2 - step) + (1 - y) * step) * chunk), chunk)
        total = (
            rows_buffer[pl.ds((3 + step) * chunk, chunk), :].astype(F32)
            + rim_rows[pl.ds((3 + step) * chunk, chunk), :].astype(F32)
            + cross_sums[step].astype(F32)
        )
        latents[here, :] = (latents[here, :].astype(F32) + gate_ref[...] * total).astype(BF16)
        store = pltpu.make_async_copy(
            latents.at[here, :], out_hbm.at[here, :], local_sem.at[step]
        )
        store.start()
        stores.append(store)
    for store in stores:
        store.wait()
    for copy in sums + last:
        copy.wait_send()
    for side in range(2):

        @pl.when((last_group if side == 0 else first_group) == 0)
        def _():
            for slot in range(8):
                tile_copy(side, slot).wait_send()


def on_device(
    latents,
    mod_shift,
    mod_scale,
    mod_gate,
    packed_weight,
    query_gain,
    key_gain,
    output_weight,
    cached,
    active_tiles,
    active_count,
    window_tiles,
    window_count,
):
    rows, width = latents.shape
    groups, tiles, window = window_tiles.shape
    share = cached.shape[1]
    heads = share // HD
    slab = cached.shape[0]
    tile = slab // tiles
    chunk = tile // 4
    assert width == 4 * share and tiles == 3 and rows == 3 * chunk and slab == 4 * rows
    anywhere = pl.BlockSpec(memory_space=pl.ANY)
    vmem = pl.BlockSpec(memory_space=pltpu.VMEM)
    smem = pl.BlockSpec(memory_space=pltpu.SMEM)
    dma = pltpu.SemaphoreType.DMA
    return pl.pallas_call(
        functools.partial(kernel, (groups, heads, tile, width, window)),
        out_shape=jax.ShapeDtypeStruct((rows, width), BF16),
        in_specs=[
            anywhere,
            vmem,
            vmem,
            vmem,
            anywhere,
            vmem,
            vmem,
            anywhere,
            anywhere,
            smem,
            smem,
            smem,
            smem,
        ],
        out_specs=anywhere,
        scratch_shapes=[
            pltpu.VMEM((rows, width), BF16),
            pltpu.VMEM((slab, width), BF16),
            pltpu.VMEM((width, 3 * share), BF16),
            pltpu.VMEM((slab, share), BF16),
            pltpu.VMEM((slab, 2 * share), BF16),
            pltpu.VMEM((2, 8, chunk, 2 * share), BF16),
            pltpu.VMEM((2, 2, tile, 2 * share), BF16),
            pltpu.VMEM((8 * chunk, width), BF16),
            pltpu.VMEM((slab, share), F32),
            pltpu.VMEM((slab, share), F32),
            pltpu.VMEM((slab, share), BF16),
            pltpu.VMEM((share, width), BF16),
            pltpu.VMEM((3, chunk, width), BF16),
            pltpu.SMEM((24,), F32),
            dma((6,)),
            dma((3,)),
            dma((3,)),
            dma((3,)),
            dma((3,)),
            dma((3,)),
            dma((3,)),
            dma((2, 8)),
            dma((2, 8)),
            dma((4,)),
            dma((4,)),
            dma((6,)),
            dma((6,)),
            dma((3,)),
            dma((3,)),
            pltpu.SemaphoreType.REGULAR,
        ],
        compiler_params=pltpu.CompilerParams(
            collective_id=0, has_side_effects=True, vmem_limit_bytes=VMEM_LIMIT
        ),
    )(
        latents,
        mod_shift[None],
        mod_scale[None],
        mod_gate[None],
        packed_weight,
        query_gain[None],
        key_gain[None],
        output_weight,
        cached,
        active_tiles,
        active_count,
        window_tiles.transpose(2, 1, 0),
        window_count,
    )


VMEM_LIMIT = 64 * 1024 * 1024


def solution(mesh):
    in_specs = (
        P(("frame", "head"), None),
        P(),
        P(),
        P(),
        P(None, "head"),
        P(),
        P(),
        P("head", None),
        P("frame", "head"),
        P("frame", None),
        P("frame"),
        P(),
        P("frame", None),
    )
    return jax.shard_map(
        on_device,
        mesh=mesh,
        in_specs=in_specs,
        out_specs=P(("frame", "head"), None),
        check_vma=False,
    )
```

```python
import functools
import math

import jax
import jax.numpy as jnp
from jax import lax
from jax.experimental import pallas as pl
from jax.experimental.pallas import tpu as pltpu
from jax.sharding import PartitionSpec as P

HD = 128
ROW = 4
BF16 = jnp.bfloat16
F32 = jnp.float32
MESH = pl.DeviceIdType.MESH


def kernel(
    sizes,
    latents_hbm,
    shift_ref,
    scale_ref,
    gate_ref,
    weight_hbm,
    query_gain_ref,
    key_gain_ref,
    out_weight_hbm,
    cached_hbm,
    active_tiles_ref,
    active_count_ref,
    window_tiles_ref,
    window_count_ref,
    out_hbm,
    latents,
    rows_buffer,
    weight,
    queries,
    bank,
    rim_send,
    rim,
    rim_rows,
    numerator,
    totals,
    attended,
    out_weight,
    cross_sums,
    masks,
    local_sem,
    near_sib_send,
    near_sib_recv,
    cross_send,
    cross_recv,
    pass_send,
    pass_recv,
    rim_send_sem,
    rim_recv_sem,
    rim_first_send,
    rim_first_recv,
    rim_pass_send,
    rim_pass_recv,
    sums_send,
    sums_recv,
    last_send,
    last_recv,
    free_sem,
):
    groups, heads, tile, width, window = sizes
    share = heads * HD
    chunk = tile // 4
    rows = 3 * chunk
    g = lax.axis_index("frame")
    h = lax.axis_index("head")
    y = h // 2
    c = h % 2
    sibling = y * 2 + (1 - c)
    cross = (1 - y) * 2 + c
    right = (g + 1) % groups
    left = (g + groups - 1) % groups
    left_edge = (ROW - g % ROW) // ROW
    right_edge = (g % ROW + 1) // ROW
    left_partner = (left, h + left_edge * (cross - h))
    right_partner = (right, h + right_edge * (cross - h))
    edge_side = right_edge
    first_group = (groups - g) // groups
    last_group = (g + 1) // groups
    edge_here = left_edge - first_group + right_edge - last_group

    def aligned(start):
        return pl.multiple_of(start, chunk)

    def far_place(step, core):
        return aligned((6 + 2 * step + core) * chunk)

    load_latents = pltpu.make_async_copy(latents_hbm, latents, local_sem.at[0])
    load_latents.start()
    parts = 3
    part_width = 3 * share // parts
    load_weight = [
        pltpu.make_async_copy(
            weight_hbm.at[:, pl.ds(part * part_width, part_width)],
            weight.at[:, pl.ds(part * part_width, part_width)],
            local_sem.at[1 + part],
        )
        for part in range(parts)
    ]
    for load in load_weight:
        load.start()
    load_out_weight = pltpu.make_async_copy(out_weight_hbm, out_weight, local_sem.at[4])
    load_cached = pltpu.make_async_copy(cached_hbm, attended, local_sem.at[5])

    barrier = pltpu.get_barrier_semaphore()
    for partner, absent in (
        ((g, sibling), 0),
        ((g, cross), 0),
        (left_partner, first_group),
        (right_partner, last_group),
    ):

        @pl.when(absent == 0)
        def _():
            pl.semaphore_signal(barrier, inc=1, device_id=partner, device_id_type=MESH)

    load_latents.wait()
    mine_at = []
    for step in range(3):
        mine = (1 - y) * (2 - step) + y * step
        x = latents[pl.ds(aligned(mine * chunk), chunk), :].astype(F32)
        centred = x - jnp.mean(x, axis=-1, keepdims=True)
        variance = jnp.mean(centred * centred, axis=-1, keepdims=True)
        normed = (
            centred * lax.rsqrt(variance + 1e-06) * (1.0 + scale_ref[...]) + shift_ref[...]
        ).astype(BF16)
        place = pl.ds(aligned(c * rows + mine * chunk), chunk)
        rows_buffer[place, :] = normed
        mine_at.append(place)

    pl.semaphore_wait(barrier, 4 - first_group - last_group)
    to_sibling, to_cross = [], []
    for step, place in enumerate(mine_at):
        over = pltpu.make_async_remote_copy(
            src_ref=rows_buffer.at[place, :],
            dst_ref=rows_buffer.at[pl.ds(far_place(step, c), chunk), :],
            send_sem=cross_send.at[step],
            recv_sem=cross_recv.at[step],
            device_id=(g, cross),
            device_id_type=MESH,
        )
        over.start()
        to_cross.append(over)
        beside = pltpu.make_async_remote_copy(
            src_ref=rows_buffer.at[place, :],
            dst_ref=rows_buffer.at[place, :],
            send_sem=near_sib_send.at[step],
            recv_sem=near_sib_recv.at[step],
            device_id=(g, sibling),
            device_id_type=MESH,
        )
        beside.start()
        to_sibling.append(beside)

    def rim_tiles(reader, owner):
        used = [jnp.int32(0)] * 3
        for j in range(3):
            for w in range(window):
                entry = window_tiles_ref[w, j, reader]
                for t in range(3):
                    used[t] = used[t] | (entry == owner * 3 + t).astype(jnp.int32)
        spare = jnp.where(used[1] == 0, 1, jnp.where(used[0] == 0, 0, 2))
        return jnp.where(spare == 0, 1, 0), jnp.where(spare == 2, 1, 2)

    send_tiles = [rim_tiles(right, g), rim_tiles(left, g)]
    recv_tiles = [rim_tiles(g, left), rim_tiles(g, right)]
    candidates = [g * 3, g * 3 + 1, g * 3 + 2]
    for side, owner in ((0, left), (1, right)):
        candidates += [owner * 3 + recv_tiles[side][0], owner * 3 + recv_tiles[side][1]]
    named = []
    for j in range(3):
        hits = [jnp.int32(0)] * 7
        for w in range(window):
            entry = window_tiles_ref[w, j, g]
            inside = (w < window_count_ref[0, j]).astype(jnp.int32)
            for k in range(7):
                hits[k] = hits[k] + inside * (entry == candidates[k]).astype(jnp.int32)
        named.append(hits)
    for t in range(3):
        holds = [
            ((active_tiles_ref[0, j] == t) & (j < active_count_ref[0])).astype(jnp.int32)
            for j in range(3)
        ]
        for k in range(7):
            masks[t * 8 + k] = sum(holds[j] * named[j][k] for j in range(3)).astype(F32)
        masks[t * 8 + 7] = sum(holds).astype(F32)

    def head_norm(vectors, gain_ref):
        mean_square = jnp.mean(vectors * vectors, axis=-1, keepdims=True)
        return (vectors * lax.rsqrt(mean_square + 1e-06) * gain_ref[...]).astype(BF16)

    pair = 2 * 3 * HD
    bank_pair = 4 * HD

    def columns_of(head):
        at = head // 2 * bank_pair + head % 2 * HD
        return (
            pl.ds(pl.multiple_of(head * HD, HD), HD),
            pl.ds(pl.multiple_of(at, HD), HD),
            pl.ds(pl.multiple_of(at + 2 * HD, HD), HD),
        )

    def project(block_at, places, after=None):
        def body(step, carry):
            columns = pl.ds(pl.multiple_of(step * pair, pair), pair)
            packed = jnp.dot(rows_buffer[block_at, :], weight[:, columns], preferred_element_type=F32)
            for half in range(2):
                at = half * 3 * HD
                head = step * 2 + half
                query_columns, key_columns, value_columns = columns_of(head)
                q = head_norm(packed[:, at : at + HD], query_gain_ref)
                k = head_norm(packed[:, at + HD : at + 2 * HD], key_gain_ref)
                v = packed[:, at + 2 * HD : at + 3 * HD].astype(BF16)
                for first, place, count in places:
                    queries[pl.ds(place, count), query_columns] = q[first : first + count]
                    bank[pl.ds(place, count), key_columns] = k[first : first + count]
                    bank[pl.ds(place, count), value_columns] = v[first : first + count]
            if after is not None:
                after(step)
            return carry

        lax.fori_loop(0, heads // 2, body, 0)

    order = ((0, 0), (0, 1), (0, 2), (1, 1), (0, 3), (1, 2), (1, 0), (1, 3))

    def quarter_of(slot, chip):
        second, quarter = order[slot]
        return second + chip * (1 - 2 * second), quarter + chip * (3 - 2 * quarter)

    def row_place(piece):
        chip, inside = piece // 6, piece % 6
        away = (chip + y) % 2
        number = inside % 3
        step = y * (2 - number) + (1 - y) * number
        return aligned(
            (1 - away) * inside * chunk + away * (6 + 2 * step + inside // 3) * chunk
        )

    half_width = width // 2

    def tile_copy(side, slot):
        second, quarter = quarter_of(slot, y)
        return pltpu.make_async_remote_copy(
            src_ref=rim_send.at[side, slot],
            dst_ref=rim.at[side, second, pl.ds(aligned(quarter * chunk), chunk), :],
            send_sem=rim_send_sem.at[side, slot],
            recv_sem=rim_recv_sem.at[side, slot],
            device_id=(right if side == 0 else left, h),
            device_id_type=MESH,
        )

    def edge_copy(side, slot):
        stage, half = slot // 2, slot % 2
        target = left + (1 - side) * (right - left)
        return pltpu.make_async_remote_copy(
            src_ref=rim_send.at[side, slot],
            dst_ref=rim_rows.at[
                pl.ds(aligned((2 * stage + c) * chunk), chunk),
                pl.ds(half * half_width, half_width),
            ],
            send_sem=rim_send_sem.at[side, slot],
            recv_sem=rim_recv_sem.at[side, slot],
            device_id=(target, cross),
            device_id_type=MESH,
        )

    def edge_pass(stage):
        here = pl.ds(aligned((2 * stage + c) * chunk), chunk)
        return pltpu.make_async_remote_copy(
            src_ref=rim_rows.at[here, :],
            dst_ref=rim_rows.at[here, :],
            send_sem=rim_pass_send.at[stage],
            recv_sem=rim_pass_recv.at[stage],
            device_id=(g, sibling),
            device_id_type=MESH,
        )

    def takes_high(side, second):
        first_tile, second_tile = send_tiles[side]
        return jnp.where(second == 0, first_tile, second_tile - 1) == 1

    def first_copy(side, slot, step):
        second, quarter = quarter_of(slot, y)
        columns = pl.ds(pl.multiple_of(step * bank_pair, bank_pair), bank_pair)
        return pltpu.make_async_remote_copy(
            src_ref=rim_send.at[side, slot, :, columns],
            dst_ref=rim.at[side, second, pl.ds(aligned(quarter * chunk), chunk), columns],
            send_sem=rim_first_send.at[side, slot, step],
            recv_sem=rim_first_recv.at[side, slot, step],
            device_id=(right if side == 0 else left, h),
            device_id_type=MESH,
        )

    def send_first_tiles(step):
        columns = pl.ds(pl.multiple_of(step * bank_pair, bank_pair), bank_pair)
        for side in range(2):
            edge = right_edge if side == 0 else left_edge

            @pl.when(edge == 0)
            def _():
                for slot in range(2):
                    second, quarter = quarter_of(slot, y)
                    low = pl.ds(aligned((4 * second + quarter) * chunk), chunk)
                    high = pl.ds(aligned((4 * second + quarter + 4) * chunk), chunk)
                    rim_send[side, slot, :, columns] = jnp.where(
                        takes_high(side, second), bank[high, columns], bank[low, columns]
                    )
                    first_copy(side, slot, step).start()

    def send_tiles_of(stage):
        for side in range(2):
            edge = right_edge if side == 0 else left_edge

            @pl.when(edge == 0)
            def _():
                for slot in (2 * stage, 2 * stage + 1):
                    second, quarter = quarter_of(slot, y)
                    low = bank[pl.ds(aligned((4 * second + quarter) * chunk), chunk), :]
                    high = bank[pl.ds(aligned((4 * second + quarter + 4) * chunk), chunk), :]
                    rim_send[side, slot] = jnp.where(takes_high(side, second), high, low)
                    tile_copy(side, slot).start()

    def send_rows_of(stage):
        for side in range(2):
            edge = right_edge if side == 0 else left_edge

            @pl.when(edge - (last_group if side == 0 else first_group) == 1)
            def _():
                second, quarter = (
                    (1 - c) * even + c * odd
                    for even, odd in zip(quarter_of(2 * stage, y), quarter_of(2 * stage + 1, y))
                )
                low = row_place(4 * second + quarter)
                high = row_place(4 * second + quarter + 4)
                for half in range(2):
                    columns = pl.ds(half * half_width, half_width)
                    rim_send[side, 2 * stage + half] = jnp.where(
                        takes_high(side, second),
                        rows_buffer[pl.ds(high, chunk), columns],
                        rows_buffer[pl.ds(low, chunk), columns],
                    )
                    edge_copy(side, 2 * stage + half).start()

    def wait_rim(slots):
        for side in range(2):
            edge = left_edge if side == 0 else right_edge

            @pl.when(edge == 0)
            def _():
                for slot in slots:
                    if slot < 2:
                        for step in range(heads // 2):
                            first_copy(side, slot, step).wait_recv()
                    else:
                        tile_copy(side, slot).wait_recv()

    def pass_edge(stage):
        @pl.when(edge_here == 1)
        def _():
            for half in range(2):
                edge_copy(edge_side, 2 * stage + half).wait_recv()
            edge_pass(stage).start()

    def project_edge(stage):
        @pl.when(edge_here == 1)
        def _():
            edge_pass(stage).wait_recv()
            places = []
            for core in range(2):
                second, quarter = quarter_of(2 * stage + core, 1 - y)
                places.append((core * chunk, second, aligned(quarter * chunk)))

            def body(step, carry):
                for head in (2 * step, 2 * step + 1):
                    columns = pl.ds(pl.multiple_of(head * 3 * HD + HD, HD), 2 * HD)
                    packed = jnp.dot(
                        rim_rows[pl.ds(2 * stage * chunk, 2 * chunk), :],
                        weight[:, columns],
                        preferred_element_type=F32,
                    )
                    k = head_norm(packed[:, :HD], key_gain_ref)
                    v = packed[:, HD:].astype(BF16)
                    _, key_columns, value_columns = columns_of(head)
                    for first, second, place in places:
                        there = pl.ds(place, chunk)
                        rim[edge_side, second, there, key_columns] = k[first : first + chunk]
                        rim[edge_side, second, there, value_columns] = v[first : first + chunk]
                return carry

            lax.fori_loop(0, heads // 2, body, 0)

    log_scale = math.log2(math.e) / math.sqrt(HD)
    triple = math.gcd(heads, 3)
    near_tile = y * 2
    far_tile = (1 - y) * 2

    def attend(q, keys, values, names):
        scores = lax.dot_general(q, keys, (((1,), (1,)), ((), ())), preferred_element_type=F32)
        weights = jnp.exp2(scores * log_scale)
        weights = jnp.concatenate(
            [weights[:, k * tile : (k + 1) * tile] * name for k, name in enumerate(names)], axis=1
        )
        total = weights[:, :HD]
        for at in range(HD, weights.shape[1], HD):
            total = total + weights[:, at : at + HD]
        return jnp.dot(weights.astype(BF16), values, preferred_element_type=F32), total

    def over_heads(work, unroll):
        def body(step, carry):
            for inner in range(unroll):
                work(step * unroll + inner)
            return carry

        lax.fori_loop(0, heads // unroll, body, 0)

    def tile_pairs(t, own, phases, fresh, head):
        here = pl.ds(aligned(t * tile), tile)
        columns, key_columns, value_columns = columns_of(head)
        keys, values, names = [], [], []
        for first, count in own:
            there = pl.ds(aligned(first * tile), count * tile)
            keys.append(bank[there, key_columns])
            values.append(bank[there, value_columns])
            names += [masks[t * 8 + first + k] for k in range(count)]
        for phase in phases:
            for side in range(2):
                edge = left_edge if side == 0 else right_edge
                second = (y + edge + phase) % 2
                keys.append(rim[side, second, :, key_columns])
                values.append(rim[side, second, :, value_columns])
                names.append(masks[t * 8 + 3 + 2 * side + second])
        out, total = attend(
            queries[here, columns],
            jnp.concatenate(keys, axis=0) if len(keys) > 1 else keys[0],
            jnp.concatenate(values, axis=0) if len(values) > 1 else values[0],
            names,
        )
        if not fresh:
            out, total = numerator[here, columns] + out, totals[here, columns] + total
        if 1 not in phases:
            numerator[here, columns] = out
            totals[here, columns] = total
        else:
            slot_out = (out / jnp.sum(total, axis=-1, keepdims=True)).astype(BF16)
            attended[here, columns] = jnp.where(
                masks[t * 8 + 7] > 0.5, slot_out, attended[here, columns]
            )

    @pl.when(first_group + last_group == 1)
    def _():
        rim[edge_side] = jnp.zeros(rim.shape[1:], BF16)

    for load in load_weight:
        load.wait()
    load_out_weight.start()
    load_cached.start()
    for copy in to_sibling:
        copy.wait_recv()
    send_rows_of(0)
    project(
        pl.ds(0, 2 * rows), [(0, aligned(y * 2 * rows), 2 * rows)], after=send_first_tiles
    )
    passed = []
    for step in range(3):
        to_cross[step].wait_recv()
        onward = pltpu.make_async_remote_copy(
            src_ref=rows_buffer.at[pl.ds(far_place(step, c), chunk), :],
            dst_ref=rows_buffer.at[pl.ds(far_place(step, c), chunk), :],
            send_sem=pass_send.at[step],
            recv_sem=pass_recv.at[step],
            device_id=(g, sibling),
            device_id_type=MESH,
        )
        onward.start()
        passed.append(onward)
        onward.wait_recv()
        send_rows_of(step + 1)
        theirs = y * (2 - step) + (1 - y) * step
        start = (1 - y) * 2 * rows + theirs * chunk
        project(
            pl.ds(far_place(step, 0), 2 * chunk),
            [(0, aligned(start), chunk), (chunk, aligned(start + rows), chunk)],
        )
        send_tiles_of(step + 1)
        pass_edge(step)
        if step == 0:
            over_heads(lambda head: tile_pairs(near_tile, [(near_tile, 1)], (), True, head), heads)
        elif step == 1:
            over_heads(lambda head: tile_pairs(1, [(y, 2)], (), True, head), triple)
        else:
            over_heads(lambda head: tile_pairs(far_tile, [(0, 3)], (), True, head), 2)
        project_edge(step)
    pass_edge(3)
    wait_rim((0, 1, 2, 4))
    over_heads(lambda head: tile_pairs(far_tile, [], (0,), False, head), heads)
    load_out_weight.wait()
    load_cached.wait()
    for copies in (to_sibling, to_cross, passed):
        for copy in copies:
            copy.wait_send()
    wait_rim((3, 5, 6, 7))
    project_edge(3)

    @pl.when(edge_here == 1)
    def _():
        for stage in range(4):
            edge_pass(stage).wait_send()

    pl.semaphore_signal(free_sem, inc=1, device_id=(g, sibling), device_id_type=MESH)
    over_heads(lambda head: tile_pairs(far_tile, [], (1,), False, head), heads)
    pl.semaphore_wait(free_sem, 1)

    def partial_sums(first, second):
        both = jnp.concatenate(
            [attended[pl.ds(aligned(first), chunk), :], attended[pl.ds(aligned(second), chunk), :]],
            axis=0,
        )
        return jnp.dot(both, out_weight[...], preferred_element_type=F32).astype(BF16)

    sums = []

    def project_out(slot, step, chip, chunk_at):
        owner = chip * 2 * rows + chunk_at * chunk
        both = partial_sums(owner + c * rows, owner + (1 - c) * rows)
        half = slot // 3
        rows_buffer[pl.ds((3 * half + step) * chunk, chunk), :] = both[:chunk]
        rows_buffer[pl.ds((6 + slot) * chunk, chunk), :] = both[chunk:]
        copy = pltpu.make_async_remote_copy(
            src_ref=rows_buffer.at[pl.ds((6 + slot) * chunk, chunk), :],
            dst_ref=rim_rows.at[pl.ds(slot * chunk, chunk), :],
            send_sem=sums_send.at[slot],
            recv_sem=sums_recv.at[slot],
            device_id=(g, sibling),
            device_id_type=MESH,
        )
        copy.start()
        sums.append(copy)

    last = []

    def send_last(step):
        sums[step].wait_recv()
        here = pl.ds(step * chunk, chunk)
        kept = rows_buffer[here, :].astype(F32)
        rows_buffer[here, :] = (kept + rim_rows[here, :].astype(F32)).astype(BF16)
        copy = pltpu.make_async_remote_copy(
            src_ref=rows_buffer.at[pl.ds(step * chunk, chunk), :],
            dst_ref=cross_sums.at[step],
            send_sem=last_send.at[step],
            recv_sem=last_recv.at[step],
            device_id=(g, cross),
            device_id_type=MESH,
        )
        copy.start()
        last.append(copy)

    for step in range(3):
        project_out(step, step, 1 - y, (1 - y) * (2 - step) + y * step)
        if step == 0:
            over_heads(
                lambda head: tile_pairs(1, [(far_tile, 1)], (0, 1), False, head), 2
            )
        send_last(step)
    over_heads(
        lambda head: tile_pairs(near_tile, [(1, 1), (far_tile, 1)], (0, 1), False, head), 2
    )
    for step in range(3):
        project_out(3 + step, step, y, y * (2 - step) + (1 - y) * step)
    stores = []
    for step in range(3):
        sums[3 + step].wait_recv()
        last[step].wait_recv()
        here = pl.ds(aligned((y * (2 - step) + (1 - y) * step) * chunk), chunk)
        total = (
            rows_buffer[pl.ds((3 + step) * chunk, chunk), :].astype(F32)
            + rim_rows[pl.ds((3 + step) * chunk, chunk), :].astype(F32)
            + cross_sums[step].astype(F32)
        )
        latents[here, :] = (latents[here, :].astype(F32) + gate_ref[...] * total).astype(BF16)
        store = pltpu.make_async_copy(
            latents.at[here, :], out_hbm.at[here, :], local_sem.at[step]
        )
        store.start()
        stores.append(store)
    for store in stores:
        store.wait()
    for copy in sums + last:
        copy.wait_send()
    for side in range(2):

        @pl.when((last_group if side == 0 else first_group) == 0)
        def _():
            for slot in range(2, 8):
                tile_copy(side, slot).wait_send()

        edge = right_edge if side == 0 else left_edge

        @pl.when(edge == 0)
        def _():
            for slot in range(2):
                for step in range(heads // 2):
                    first_copy(side, slot, step).wait_send()

        @pl.when(edge - (last_group if side == 0 else first_group) == 1)
        def _():
            for slot in range(2):
                edge_copy(side, slot).wait_send()


def on_device(
    latents,
    mod_shift,
    mod_scale,
    mod_gate,
    packed_weight,
    query_gain,
    key_gain,
    output_weight,
    cached,
    active_tiles,
    active_count,
    window_tiles,
    window_count,
):
    rows, width = latents.shape
    groups, tiles, window = window_tiles.shape
    share = cached.shape[1]
    heads = share // HD
    slab = cached.shape[0]
    tile = slab // tiles
    chunk = tile // 4
    assert width == 4 * share and tiles == 3 and rows == 3 * chunk and slab == 4 * rows
    anywhere = pl.BlockSpec(memory_space=pl.ANY)
    vmem = pl.BlockSpec(memory_space=pltpu.VMEM)
    smem = pl.BlockSpec(memory_space=pltpu.SMEM)
    dma = pltpu.SemaphoreType.DMA
    return pl.pallas_call(
        functools.partial(kernel, (groups, heads, tile, width, window)),
        out_shape=jax.ShapeDtypeStruct((rows, width), BF16),
        in_specs=[
            anywhere,
            vmem,
            vmem,
            vmem,
            anywhere,
            vmem,
            vmem,
            anywhere,
            anywhere,
            smem,
            smem,
            smem,
            smem,
        ],
        out_specs=anywhere,
        scratch_shapes=[
            pltpu.VMEM((rows, width), BF16),
            pltpu.VMEM((slab, width), BF16),
            pltpu.VMEM((width, 3 * share), BF16),
            pltpu.VMEM((slab, share), BF16),
            pltpu.VMEM((slab, 2 * share), BF16),
            pltpu.VMEM((2, 8, chunk, 2 * share), BF16),
            pltpu.VMEM((2, 2, tile, 2 * share), BF16),
            pltpu.VMEM((8 * chunk, width), BF16),
            pltpu.VMEM((slab, share), F32),
            pltpu.VMEM((slab, share), F32),
            pltpu.VMEM((slab, share), BF16),
            pltpu.VMEM((share, width), BF16),
            pltpu.VMEM((3, chunk, width), BF16),
            pltpu.SMEM((24,), F32),
            dma((6,)),
            dma((3,)),
            dma((3,)),
            dma((3,)),
            dma((3,)),
            dma((3,)),
            dma((3,)),
            dma((2, 8)),
            dma((2, 8)),
            dma((2, 2, heads // 2)),
            dma((2, 2, heads // 2)),
            dma((4,)),
            dma((4,)),
            dma((6,)),
            dma((6,)),
            dma((3,)),
            dma((3,)),
            pltpu.SemaphoreType.REGULAR,
        ],
        compiler_params=pltpu.CompilerParams(
            collective_id=0, has_side_effects=True, vmem_limit_bytes=VMEM_LIMIT
        ),
    )(
        latents,
        mod_shift[None],
        mod_scale[None],
        mod_gate[None],
        packed_weight,
        query_gain[None],
        key_gain[None],
        output_weight,
        cached,
        active_tiles,
        active_count,
        window_tiles.transpose(2, 1, 0),
        window_count,
    )


VMEM_LIMIT = 64 * 1024 * 1024


def solution(mesh):
    in_specs = (
        P(("frame", "head"), None),
        P(),
        P(),
        P(),
        P(None, "head"),
        P(),
        P(),
        P("head", None),
        P("frame", "head"),
        P("frame", None),
        P("frame"),
        P(),
        P("frame", None),
    )
    return jax.shard_map(
        on_device,
        mesh=mesh,
        in_specs=in_specs,
        out_specs=P(("frame", "head"), None),
        check_vma=False,
    )
```

```python
import functools
import math

import jax
import jax.numpy as jnp
from jax import lax
from jax.experimental import pallas as pl
from jax.experimental.pallas import tpu as pltpu
from jax.sharding import PartitionSpec as P

HD = 128
ROW = 4
BF16 = jnp.bfloat16
F32 = jnp.float32
MESH = pl.DeviceIdType.MESH


def kernel(
    sizes,
    latents_hbm,
    shift_ref,
    scale_ref,
    gate_ref,
    weight_hbm,
    query_gain_ref,
    key_gain_ref,
    out_weight_hbm,
    cached_hbm,
    active_tiles_ref,
    active_count_ref,
    window_tiles_ref,
    window_count_ref,
    out_hbm,
    latents,
    rows_buffer,
    weight,
    queries,
    bank,
    rim_send,
    rim,
    rim_rows,
    numerator,
    totals,
    attended,
    out_weight,
    cross_sums,
    masks,
    local_sem,
    near_sib_send,
    near_sib_recv,
    cross_send,
    cross_recv,
    pass_send,
    pass_recv,
    rim_send_sem,
    rim_recv_sem,
    rim_first_send,
    rim_first_recv,
    rim_pass_send,
    rim_pass_recv,
    sums_send,
    sums_recv,
    last_send,
    last_recv,
    free_sem,
):
    groups, heads, tile, width, window = sizes
    share = heads * HD
    chunk = tile // 4
    rows = 3 * chunk
    g = lax.axis_index("frame")
    h = lax.axis_index("head")
    y = h // 2
    c = h % 2
    sibling = y * 2 + (1 - c)
    cross = (1 - y) * 2 + c
    right = (g + 1) % groups
    left = (g + groups - 1) % groups
    left_edge = (ROW - g % ROW) // ROW
    right_edge = (g % ROW + 1) // ROW
    left_partner = (left, h + left_edge * (cross - h))
    right_partner = (right, h + right_edge * (cross - h))
    edge_side = right_edge
    first_group = (groups - g) // groups
    last_group = (g + 1) // groups
    edge_here = left_edge - first_group + right_edge - last_group

    def aligned(start):
        return pl.multiple_of(start, chunk)

    def far_place(step, core):
        return aligned((6 + 2 * step + core) * chunk)

    load_latents = pltpu.make_async_copy(latents_hbm, latents, local_sem.at[0])
    load_latents.start()
    parts = 3
    part_width = 3 * share // parts
    load_weight = [
        pltpu.make_async_copy(
            weight_hbm.at[:, pl.ds(part * part_width, part_width)],
            weight.at[:, pl.ds(part * part_width, part_width)],
            local_sem.at[1 + part],
        )
        for part in range(parts)
    ]
    for load in load_weight:
        load.start()
    load_out_weight = pltpu.make_async_copy(out_weight_hbm, out_weight, local_sem.at[4])
    load_cached = pltpu.make_async_copy(cached_hbm, attended, local_sem.at[5])

    barrier = pltpu.get_barrier_semaphore()
    for partner, absent in (
        ((g, sibling), 0),
        ((g, cross), 0),
        (left_partner, first_group),
        (right_partner, last_group),
    ):

        @pl.when(absent == 0)
        def _():
            pl.semaphore_signal(barrier, inc=1, device_id=partner, device_id_type=MESH)

    load_latents.wait()
    mine_at = []
    for step in range(3):
        mine = (1 - y) * (2 - step) + y * step
        x = latents[pl.ds(aligned(mine * chunk), chunk), :].astype(F32)
        centred = x - jnp.mean(x, axis=-1, keepdims=True)
        variance = jnp.mean(centred * centred, axis=-1, keepdims=True)
        normed = (
            centred * lax.rsqrt(variance + 1e-06) * (1.0 + scale_ref[...]) + shift_ref[...]
        ).astype(BF16)
        place = pl.ds(aligned(c * rows + mine * chunk), chunk)
        rows_buffer[place, :] = normed
        mine_at.append(place)

    pl.semaphore_wait(barrier, 4 - first_group - last_group)
    to_sibling, to_cross = [], []
    for step, place in enumerate(mine_at):
        over = pltpu.make_async_remote_copy(
            src_ref=rows_buffer.at[place, :],
            dst_ref=rows_buffer.at[pl.ds(far_place(step, c), chunk), :],
            send_sem=cross_send.at[step],
            recv_sem=cross_recv.at[step],
            device_id=(g, cross),
            device_id_type=MESH,
        )
        over.start()
        to_cross.append(over)
        beside = pltpu.make_async_remote_copy(
            src_ref=rows_buffer.at[place, :],
            dst_ref=rows_buffer.at[place, :],
            send_sem=near_sib_send.at[step],
            recv_sem=near_sib_recv.at[step],
            device_id=(g, sibling),
            device_id_type=MESH,
        )
        beside.start()
        to_sibling.append(beside)

    def rim_tiles(reader, owner):
        used = [jnp.int32(0)] * 3
        for j in range(3):
            for w in range(window):
                entry = window_tiles_ref[w, j, reader]
                for t in range(3):
                    used[t] = used[t] | (entry == owner * 3 + t).astype(jnp.int32)
        spare = jnp.where(used[1] == 0, 1, jnp.where(used[0] == 0, 0, 2))
        return jnp.where(spare == 0, 1, 0), jnp.where(spare == 2, 1, 2)

    send_tiles = [rim_tiles(right, g), rim_tiles(left, g)]
    recv_tiles = [rim_tiles(g, left), rim_tiles(g, right)]
    candidates = [g * 3, g * 3 + 1, g * 3 + 2]
    for side, owner in ((0, left), (1, right)):
        candidates += [owner * 3 + recv_tiles[side][0], owner * 3 + recv_tiles[side][1]]
    named = []
    for j in range(3):
        hits = [jnp.int32(0)] * 7
        for w in range(window):
            entry = window_tiles_ref[w, j, g]
            inside = (w < window_count_ref[0, j]).astype(jnp.int32)
            for k in range(7):
                hits[k] = hits[k] + inside * (entry == candidates[k]).astype(jnp.int32)
        named.append(hits)
    for t in range(3):
        holds = [
            ((active_tiles_ref[0, j] == t) & (j < active_count_ref[0])).astype(jnp.int32)
            for j in range(3)
        ]
        for k in range(7):
            masks[t * 8 + k] = sum(holds[j] * named[j][k] for j in range(3)).astype(F32)
        masks[t * 8 + 7] = sum(holds).astype(F32)

    def head_norm(vectors, gain_ref):
        mean_square = jnp.mean(vectors * vectors, axis=-1, keepdims=True)
        return (vectors * lax.rsqrt(mean_square + 1e-06) * gain_ref[...]).astype(BF16)

    pair = 2 * 3 * HD
    bank_pair = 4 * HD

    def columns_of(head):
        at = head // 2 * bank_pair + head % 2 * HD
        return (
            pl.ds(pl.multiple_of(head * HD, HD), HD),
            pl.ds(pl.multiple_of(at, HD), HD),
            pl.ds(pl.multiple_of(at + 2 * HD, HD), HD),
        )

    def project(block_at, places, after=None):
        def body(step, carry):
            columns = pl.ds(pl.multiple_of(step * pair, pair), pair)
            packed = jnp.dot(rows_buffer[block_at, :], weight[:, columns], preferred_element_type=F32)
            for half in range(2):
                at = half * 3 * HD
                head = step * 2 + half
                query_columns, key_columns, value_columns = columns_of(head)
                q = head_norm(packed[:, at : at + HD], query_gain_ref)
                k = head_norm(packed[:, at + HD : at + 2 * HD], key_gain_ref)
                v = packed[:, at + 2 * HD : at + 3 * HD].astype(BF16)
                for first, place, count in places:
                    queries[pl.ds(place, count), query_columns] = q[first : first + count]
                    bank[pl.ds(place, count), key_columns] = k[first : first + count]
                    bank[pl.ds(place, count), value_columns] = v[first : first + count]
            if after is not None:
                after(step)
            return carry

        lax.fori_loop(0, heads // 2, body, 0)

    order = ((0, 0), (0, 1), (0, 2), (1, 1), (0, 3), (1, 2), (1, 0), (1, 3))

    def quarter_of(slot, chip):
        second, quarter = order[slot]
        return second + chip * (1 - 2 * second), quarter + chip * (3 - 2 * quarter)

    def row_place(piece):
        chip, inside = piece // 6, piece % 6
        away = (chip + y) % 2
        number = inside % 3
        step = y * (2 - number) + (1 - y) * number
        return aligned(
            (1 - away) * inside * chunk + away * (6 + 2 * step + inside // 3) * chunk
        )

    half_width = width // 2

    def tile_copy(side, slot):
        second, quarter = quarter_of(slot, y)
        return pltpu.make_async_remote_copy(
            src_ref=rim_send.at[side, slot],
            dst_ref=rim.at[side, second, pl.ds(aligned(quarter * chunk), chunk), :],
            send_sem=rim_send_sem.at[side, slot],
            recv_sem=rim_recv_sem.at[side, slot],
            device_id=(right if side == 0 else left, h),
            device_id_type=MESH,
        )

    def edge_copy(side, slot):
        stage, half = slot // 2, slot % 2
        target = left + (1 - side) * (right - left)
        return pltpu.make_async_remote_copy(
            src_ref=rim_send.at[side, slot],
            dst_ref=rim_rows.at[
                pl.ds(aligned((2 * stage + c) * chunk), chunk),
                pl.ds(half * half_width, half_width),
            ],
            send_sem=rim_send_sem.at[side, slot],
            recv_sem=rim_recv_sem.at[side, slot],
            device_id=(target, cross),
            device_id_type=MESH,
        )

    def edge_pass(stage):
        here = pl.ds(aligned((2 * stage + c) * chunk), chunk)
        return pltpu.make_async_remote_copy(
            src_ref=rim_rows.at[here, :],
            dst_ref=rim_rows.at[here, :],
            send_sem=rim_pass_send.at[stage],
            recv_sem=rim_pass_recv.at[stage],
            device_id=(g, sibling),
            device_id_type=MESH,
        )

    def takes_high(side, second):
        first_tile, second_tile = send_tiles[side]
        return jnp.where(second == 0, first_tile, second_tile - 1) == 1

    def first_copy(side, slot, step):
        second, quarter = quarter_of(slot, y)
        columns = pl.ds(pl.multiple_of(step * bank_pair, bank_pair), bank_pair)
        return pltpu.make_async_remote_copy(
            src_ref=rim_send.at[side, slot, :, columns],
            dst_ref=rim.at[side, second, pl.ds(aligned(quarter * chunk), chunk), columns],
            send_sem=rim_first_send.at[side, slot, step],
            recv_sem=rim_first_recv.at[side, slot, step],
            device_id=(right if side == 0 else left, h),
            device_id_type=MESH,
        )

    def send_first_tiles(step):
        columns = pl.ds(pl.multiple_of(step * bank_pair, bank_pair), bank_pair)
        for side in range(2):
            edge = right_edge if side == 0 else left_edge

            @pl.when(edge == 0)
            def _():
                for slot in range(2):
                    second, quarter = quarter_of(slot, y)
                    low = pl.ds(aligned((4 * second + quarter) * chunk), chunk)
                    high = pl.ds(aligned((4 * second + quarter + 4) * chunk), chunk)
                    rim_send[side, slot, :, columns] = jnp.where(
                        takes_high(side, second), bank[high, columns], bank[low, columns]
                    )
                    first_copy(side, slot, step).start()

    def send_tiles_of(stage):
        for side in range(2):
            edge = right_edge if side == 0 else left_edge

            @pl.when(edge == 0)
            def _():
                for slot in (2 * stage, 2 * stage + 1):
                    second, quarter = quarter_of(slot, y)
                    low = bank[pl.ds(aligned((4 * second + quarter) * chunk), chunk), :]
                    high = bank[pl.ds(aligned((4 * second + quarter + 4) * chunk), chunk), :]
                    rim_send[side, slot] = jnp.where(takes_high(side, second), high, low)
                    tile_copy(side, slot).start()

    def send_rows_of(stage):
        for side in range(2):
            edge = right_edge if side == 0 else left_edge

            @pl.when(edge - (last_group if side == 0 else first_group) == 1)
            def _():
                second, quarter = (
                    (1 - c) * even + c * odd
                    for even, odd in zip(quarter_of(2 * stage, y), quarter_of(2 * stage + 1, y))
                )
                low = row_place(4 * second + quarter)
                high = row_place(4 * second + quarter + 4)
                for half in range(2):
                    columns = pl.ds(half * half_width, half_width)
                    rim_send[side, 2 * stage + half] = jnp.where(
                        takes_high(side, second),
                        rows_buffer[pl.ds(high, chunk), columns],
                        rows_buffer[pl.ds(low, chunk), columns],
                    )
                    edge_copy(side, 2 * stage + half).start()

    def wait_rim(slots):
        for side in range(2):
            edge = left_edge if side == 0 else right_edge

            @pl.when(edge == 0)
            def _():
                for slot in slots:
                    if slot < 2:
                        for step in range(heads // 2):
                            first_copy(side, slot, step).wait_recv()
                    else:
                        tile_copy(side, slot).wait_recv()

    def pass_edge(stage):
        @pl.when(edge_here == 1)
        def _():
            for half in range(2):
                edge_copy(edge_side, 2 * stage + half).wait_recv()
            edge_pass(stage).start()

    def project_edge(stage):
        @pl.when(edge_here == 1)
        def _():
            edge_pass(stage).wait_recv()
            places = []
            for core in range(2):
                second, quarter = quarter_of(2 * stage + core, 1 - y)
                places.append((core * chunk, second, aligned(quarter * chunk)))

            def body(step, carry):
                for head in (2 * step, 2 * step + 1):
                    columns = pl.ds(pl.multiple_of(head * 3 * HD + HD, HD), 2 * HD)
                    packed = jnp.dot(
                        rim_rows[pl.ds(2 * stage * chunk, 2 * chunk), :],
                        weight[:, columns],
                        preferred_element_type=F32,
                    )
                    k = head_norm(packed[:, :HD], key_gain_ref)
                    v = packed[:, HD:].astype(BF16)
                    _, key_columns, value_columns = columns_of(head)
                    for first, second, place in places:
                        there = pl.ds(place, chunk)
                        rim[edge_side, second, there, key_columns] = k[first : first + chunk]
                        rim[edge_side, second, there, value_columns] = v[first : first + chunk]
                return carry

            lax.fori_loop(0, heads // 2, body, 0)

    log_scale = math.log2(math.e) / math.sqrt(HD)
    triple = math.gcd(heads, 3)
    near_tile = y * 2
    far_tile = (1 - y) * 2

    def attend(q, keys, values, names):
        scores = lax.dot_general(q, keys, (((1,), (1,)), ((), ())), preferred_element_type=F32)
        weights = jnp.exp2(scores * log_scale)
        weights = jnp.concatenate(
            [weights[:, k * tile : (k + 1) * tile] * name for k, name in enumerate(names)], axis=1
        )
        total = weights[:, :HD]
        for at in range(HD, weights.shape[1], HD):
            total = total + weights[:, at : at + HD]
        return jnp.dot(weights.astype(BF16), values, preferred_element_type=F32), total

    def over_heads(work, unroll):
        def body(step, carry):
            for inner in range(unroll):
                work(step * unroll + inner)
            return carry

        lax.fori_loop(0, heads // unroll, body, 0)

    def tile_pairs(t, own, phases, fresh, head):
        here = pl.ds(aligned(t * tile), tile)
        columns, key_columns, value_columns = columns_of(head)
        keys, values, names = [], [], []
        for first, count in own:
            there = pl.ds(aligned(first * tile), count * tile)
            keys.append(bank[there, key_columns])
            values.append(bank[there, value_columns])
            names += [masks[t * 8 + first + k] for k in range(count)]
        for phase in phases:
            for side in range(2):
                edge = left_edge if side == 0 else right_edge
                second = (y + edge + phase) % 2
                keys.append(rim[side, second, :, key_columns])
                values.append(rim[side, second, :, value_columns])
                names.append(masks[t * 8 + 3 + 2 * side + second])
        out, total = attend(
            queries[here, columns],
            jnp.concatenate(keys, axis=0) if len(keys) > 1 else keys[0],
            jnp.concatenate(values, axis=0) if len(values) > 1 else values[0],
            names,
        )
        if not fresh:
            out, total = numerator[here, columns] + out, totals[here, columns] + total
        if 1 not in phases:
            numerator[here, columns] = out
            totals[here, columns] = total
        else:
            slot_out = (out / jnp.sum(total, axis=-1, keepdims=True)).astype(BF16)
            attended[here, columns] = jnp.where(
                masks[t * 8 + 7] > 0.5, slot_out, attended[here, columns]
            )

    @pl.when(first_group + last_group == 1)
    def _():
        rim[edge_side] = jnp.zeros(rim.shape[1:], BF16)

    for load in load_weight:
        load.wait()
    load_out_weight.start()
    load_cached.start()
    for copy in to_sibling:
        copy.wait_recv()
    send_rows_of(0)
    project(
        pl.ds(0, 2 * rows), [(0, aligned(y * 2 * rows), 2 * rows)], after=send_first_tiles
    )
    passed = []
    for step in range(3):
        to_cross[step].wait_recv()
        onward = pltpu.make_async_remote_copy(
            src_ref=rows_buffer.at[pl.ds(far_place(step, c), chunk), :],
            dst_ref=rows_buffer.at[pl.ds(far_place(step, c), chunk), :],
            send_sem=pass_send.at[step],
            recv_sem=pass_recv.at[step],
            device_id=(g, sibling),
            device_id_type=MESH,
        )
        onward.start()
        passed.append(onward)
        onward.wait_recv()
        send_rows_of(step + 1)
        theirs = y * (2 - step) + (1 - y) * step
        start = (1 - y) * 2 * rows + theirs * chunk
        project(
            pl.ds(far_place(step, 0), 2 * chunk),
            [(0, aligned(start), chunk), (chunk, aligned(start + rows), chunk)],
        )
        send_tiles_of(step + 1)
        pass_edge(step)
        if step == 0:
            over_heads(lambda head: tile_pairs(near_tile, [(near_tile, 1)], (), True, head), heads)
        elif step == 1:
            over_heads(lambda head: tile_pairs(1, [(y, 2)], (), True, head), triple)
        else:
            over_heads(lambda head: tile_pairs(far_tile, [(0, 3)], (), True, head), 2)
        project_edge(step)
    pass_edge(3)
    wait_rim((0, 1, 2, 4))
    over_heads(lambda head: tile_pairs(far_tile, [], (0,), False, head), heads)
    load_out_weight.wait()
    load_cached.wait()
    for copies in (to_sibling, to_cross, passed):
        for copy in copies:
            copy.wait_send()
    wait_rim((3, 5, 6, 7))
    project_edge(3)

    @pl.when(edge_here == 1)
    def _():
        for stage in range(4):
            edge_pass(stage).wait_send()

    pl.semaphore_signal(free_sem, inc=1, device_id=(g, sibling), device_id_type=MESH)
    over_heads(lambda head: tile_pairs(far_tile, [], (1,), False, head), heads)
    pl.semaphore_wait(free_sem, 1)

    def half_columns(half):
        return pl.ds(half * half_width, half_width)

    sums = {}

    def project_out(slot, step, chip, chunk_at):
        owner = chip * 2 * rows + chunk_at * chunk
        both = jnp.concatenate(
            [
                attended[pl.ds(aligned(owner + core * rows), chunk), :]
                for core in (c, 1 - c)
            ],
            axis=0,
        )
        kept = pl.ds((3 * (slot // 3) + step) * chunk, chunk)
        given = pl.ds((6 + slot) * chunk, chunk)
        for half in range(2):
            columns = half_columns(half)
            part = jnp.dot(both, out_weight[:, columns], preferred_element_type=F32).astype(BF16)
            rows_buffer[given, columns] = part[chunk:]
            copy = pltpu.make_async_remote_copy(
                src_ref=rows_buffer.at[given, columns],
                dst_ref=rim_rows.at[pl.ds(slot * chunk, chunk), columns],
                send_sem=sums_send.at[slot, half],
                recv_sem=sums_recv.at[slot, half],
                device_id=(g, sibling),
                device_id_type=MESH,
            )
            copy.start()
            sums[slot, half] = copy
            rows_buffer[kept, columns] = part[:chunk]

    last = {}

    def send_last(step):
        here = pl.ds(step * chunk, chunk)
        for half in range(2):
            columns = half_columns(half)
            sums[step, half].wait_recv()
            kept = rows_buffer[here, columns].astype(F32)
            rows_buffer[here, columns] = (kept + rim_rows[here, columns].astype(F32)).astype(BF16)
            copy = pltpu.make_async_remote_copy(
                src_ref=rows_buffer.at[here, columns],
                dst_ref=cross_sums.at[step, :, columns],
                send_sem=last_send.at[step, half],
                recv_sem=last_recv.at[step, half],
                device_id=(g, cross),
                device_id_type=MESH,
            )
            copy.start()
            last[step, half] = copy

    def far_out(step):
        project_out(step, step, 1 - y, (1 - y) * (2 - step) + y * step)

    far_out(0)
    send_last(0)
    over_heads(lambda head: tile_pairs(1, [(far_tile, 1)], (0, 1), False, head), 2)
    far_out(1)
    far_out(2)
    send_last(1)
    send_last(2)
    over_heads(
        lambda head: tile_pairs(near_tile, [(1, 1), (far_tile, 1)], (0, 1), False, head), 2
    )
    for step in range(3):
        project_out(3 + step, step, y, y * (2 - step) + (1 - y) * step)
    stores = []
    for step in range(3):
        here = pl.ds(aligned((y * (2 - step) + (1 - y) * step) * chunk), chunk)
        own = pl.ds((3 + step) * chunk, chunk)
        for half in range(2):
            columns = half_columns(half)
            sums[3 + step, half].wait_recv()
            near_sum = rows_buffer[own, columns].astype(F32) + rim_rows[own, columns].astype(F32)
            last[step, half].wait_recv()
            total = near_sum + cross_sums[step, :, columns].astype(F32)
            latents[here, columns] = (
                latents[here, columns].astype(F32) + gate_ref[:, columns] * total
            ).astype(BF16)
            store = pltpu.make_async_copy(
                latents.at[here, columns],
                out_hbm.at[here, columns],
                local_sem.at[2 * step + half],
            )
            store.start()
            stores.append(store)
    for store in stores:
        store.wait()
    for copies in (sums, last):
        for copy in copies.values():
            copy.wait_send()
    for side in range(2):

        @pl.when((last_group if side == 0 else first_group) == 0)
        def _():
            for slot in range(2, 8):
                tile_copy(side, slot).wait_send()

        edge = right_edge if side == 0 else left_edge

        @pl.when(edge == 0)
        def _():
            for slot in range(2):
                for step in range(heads // 2):
                    first_copy(side, slot, step).wait_send()

        @pl.when(edge - (last_group if side == 0 else first_group) == 1)
        def _():
            for slot in range(2):
                edge_copy(side, slot).wait_send()


def on_device(
    latents,
    mod_shift,
    mod_scale,
    mod_gate,
    packed_weight,
    query_gain,
    key_gain,
    output_weight,
    cached,
    active_tiles,
    active_count,
    window_tiles,
    window_count,
):
    rows, width = latents.shape
    groups, tiles, window = window_tiles.shape
    share = cached.shape[1]
    heads = share // HD
    slab = cached.shape[0]
    tile = slab // tiles
    chunk = tile // 4
    assert width == 4 * share and tiles == 3 and rows == 3 * chunk and slab == 4 * rows
    anywhere = pl.BlockSpec(memory_space=pl.ANY)
    vmem = pl.BlockSpec(memory_space=pltpu.VMEM)
    smem = pl.BlockSpec(memory_space=pltpu.SMEM)
    dma = pltpu.SemaphoreType.DMA
    return pl.pallas_call(
        functools.partial(kernel, (groups, heads, tile, width, window)),
        out_shape=jax.ShapeDtypeStruct((rows, width), BF16),
        in_specs=[
            anywhere,
            vmem,
            vmem,
            vmem,
            anywhere,
            vmem,
            vmem,
            anywhere,
            anywhere,
            smem,
            smem,
            smem,
            smem,
        ],
        out_specs=anywhere,
        scratch_shapes=[
            pltpu.VMEM((rows, width), BF16),
            pltpu.VMEM((slab, width), BF16),
            pltpu.VMEM((width, 3 * share), BF16),
            pltpu.VMEM((slab, share), BF16),
            pltpu.VMEM((slab, 2 * share), BF16),
            pltpu.VMEM((2, 8, chunk, 2 * share), BF16),
            pltpu.VMEM((2, 2, tile, 2 * share), BF16),
            pltpu.VMEM((8 * chunk, width), BF16),
            pltpu.VMEM((slab, share), F32),
            pltpu.VMEM((slab, share), F32),
            pltpu.VMEM((slab, share), BF16),
            pltpu.VMEM((share, width), BF16),
            pltpu.VMEM((3, chunk, width), BF16),
            pltpu.SMEM((24,), F32),
            dma((6,)),
            dma((3,)),
            dma((3,)),
            dma((3,)),
            dma((3,)),
            dma((3,)),
            dma((3,)),
            dma((2, 8)),
            dma((2, 8)),
            dma((2, 2, heads // 2)),
            dma((2, 2, heads // 2)),
            dma((4,)),
            dma((4,)),
            dma((6, 2)),
            dma((6, 2)),
            dma((3, 2)),
            dma((3, 2)),
            pltpu.SemaphoreType.REGULAR,
        ],
        compiler_params=pltpu.CompilerParams(
            collective_id=0, has_side_effects=True, vmem_limit_bytes=VMEM_LIMIT
        ),
    )(
        latents,
        mod_shift[None],
        mod_scale[None],
        mod_gate[None],
        packed_weight,
        query_gain[None],
        key_gain[None],
        output_weight,
        cached,
        active_tiles,
        active_count,
        window_tiles.transpose(2, 1, 0),
        window_count,
    )


VMEM_LIMIT = 64 * 1024 * 1024


def solution(mesh):
    in_specs = (
        P(("frame", "head"), None),
        P(),
        P(),
        P(),
        P(None, "head"),
        P(),
        P(),
        P("head", None),
        P("frame", "head"),
        P("frame", None),
        P("frame"),
        P(),
        P("frame", None),
    )
    return jax.shard_map(
        on_device,
        mesh=mesh,
        in_specs=in_specs,
        out_specs=P(("frame", "head"), None),
        check_vma=False,
    )
```

```python
import functools
import math

import jax
import jax.numpy as jnp
from jax import lax
from jax.experimental import pallas as pl
from jax.experimental.pallas import tpu as pltpu
from jax.sharding import PartitionSpec as P

HD = 128
ROW = 4
BF16 = jnp.bfloat16
F32 = jnp.float32
MESH = pl.DeviceIdType.MESH


def kernel(
    sizes,
    latents_hbm,
    shift_ref,
    scale_ref,
    gate_ref,
    weight_hbm,
    query_gain_ref,
    key_gain_ref,
    out_weight_hbm,
    cached_hbm,
    active_tiles_ref,
    active_count_ref,
    window_tiles_ref,
    window_count_ref,
    out_hbm,
    latents,
    rows_buffer,
    weight,
    queries,
    bank,
    rim_send,
    rim,
    rim_rows,
    numerator,
    totals,
    attended,
    out_weight,
    cross_sums,
    masks,
    local_sem,
    near_sib_send,
    near_sib_recv,
    cross_send,
    cross_recv,
    pass_send,
    pass_recv,
    rim_send_sem,
    rim_recv_sem,
    rim_first_send,
    rim_first_recv,
    rim_pass_send,
    rim_pass_recv,
    sums_send,
    sums_recv,
    last_send,
    last_recv,
    free_sem,
):
    groups, heads, tile, width, window = sizes
    share = heads * HD
    chunk = tile // 4
    rows = 3 * chunk
    g = lax.axis_index("frame")
    h = lax.axis_index("head")
    y = h // 2
    c = h % 2
    sibling = y * 2 + (1 - c)
    cross = (1 - y) * 2 + c
    right = (g + 1) % groups
    left = (g + groups - 1) % groups
    left_edge = (ROW - g % ROW) // ROW
    right_edge = (g % ROW + 1) // ROW
    left_partner = (left, h + left_edge * (cross - h))
    right_partner = (right, h + right_edge * (cross - h))
    edge_side = right_edge
    first_group = (groups - g) // groups
    last_group = (g + 1) // groups
    edge_here = left_edge - first_group + right_edge - last_group

    def aligned(start):
        return pl.multiple_of(start, chunk)

    def far_place(step, core):
        return aligned((6 + 2 * step + core) * chunk)

    load_latents = pltpu.make_async_copy(latents_hbm, latents, local_sem.at[0])
    load_latents.start()
    parts = 3
    part_width = 3 * share // parts
    load_weight = [
        pltpu.make_async_copy(
            weight_hbm.at[:, pl.ds(part * part_width, part_width)],
            weight.at[:, pl.ds(part * part_width, part_width)],
            local_sem.at[1 + part],
        )
        for part in range(parts)
    ]
    for load in load_weight:
        load.start()
    load_out_weight = pltpu.make_async_copy(out_weight_hbm, out_weight, local_sem.at[4])
    load_cached = pltpu.make_async_copy(cached_hbm, attended, local_sem.at[5])

    barrier = pltpu.get_barrier_semaphore()
    for partner, absent in (
        ((g, sibling), 0),
        ((g, cross), 0),
        (left_partner, first_group),
        (right_partner, last_group),
    ):

        @pl.when(absent == 0)
        def _():
            pl.semaphore_signal(barrier, inc=1, device_id=partner, device_id_type=MESH)

    load_latents.wait()
    mine_at = []
    for step in range(3):
        mine = (1 - y) * (2 - step) + y * step
        x = latents[pl.ds(aligned(mine * chunk), chunk), :].astype(F32)
        centred = x - jnp.mean(x, axis=-1, keepdims=True)
        variance = jnp.mean(centred * centred, axis=-1, keepdims=True)
        normed = (
            centred * lax.rsqrt(variance + 1e-06) * (1.0 + scale_ref[...]) + shift_ref[...]
        ).astype(BF16)
        place = pl.ds(aligned(c * rows + mine * chunk), chunk)
        rows_buffer[place, :] = normed
        mine_at.append(place)

    pl.semaphore_wait(barrier, 4 - first_group - last_group)
    to_sibling, to_cross = [], []
    for step, place in enumerate(mine_at):
        over = pltpu.make_async_remote_copy(
            src_ref=rows_buffer.at[place, :],
            dst_ref=rows_buffer.at[pl.ds(far_place(step, c), chunk), :],
            send_sem=cross_send.at[step],
            recv_sem=cross_recv.at[step],
            device_id=(g, cross),
            device_id_type=MESH,
        )
        over.start()
        to_cross.append(over)
        beside = pltpu.make_async_remote_copy(
            src_ref=rows_buffer.at[place, :],
            dst_ref=rows_buffer.at[place, :],
            send_sem=near_sib_send.at[step],
            recv_sem=near_sib_recv.at[step],
            device_id=(g, sibling),
            device_id_type=MESH,
        )
        beside.start()
        to_sibling.append(beside)

    def rim_tiles(reader, owner):
        used = [jnp.int32(0)] * 3
        for j in range(3):
            for w in range(window):
                entry = window_tiles_ref[w, j, reader]
                for t in range(3):
                    used[t] = used[t] | (entry == owner * 3 + t).astype(jnp.int32)
        spare = jnp.where(used[1] == 0, 1, jnp.where(used[0] == 0, 0, 2))
        return jnp.where(spare == 0, 1, 0), jnp.where(spare == 2, 1, 2)

    send_tiles = [rim_tiles(right, g), rim_tiles(left, g)]
    recv_tiles = [rim_tiles(g, left), rim_tiles(g, right)]
    candidates = [g * 3, g * 3 + 1, g * 3 + 2]
    for side, owner in ((0, left), (1, right)):
        candidates += [owner * 3 + recv_tiles[side][0], owner * 3 + recv_tiles[side][1]]
    named = []
    for j in range(3):
        hits = [jnp.int32(0)] * 7
        for w in range(window):
            entry = window_tiles_ref[w, j, g]
            inside = (w < window_count_ref[0, j]).astype(jnp.int32)
            for k in range(7):
                hits[k] = hits[k] + inside * (entry == candidates[k]).astype(jnp.int32)
        named.append(hits)
    for t in range(3):
        holds = [
            ((active_tiles_ref[0, j] == t) & (j < active_count_ref[0])).astype(jnp.int32)
            for j in range(3)
        ]
        for k in range(7):
            masks[t * 8 + k] = sum(holds[j] * named[j][k] for j in range(3)).astype(F32)
        masks[t * 8 + 7] = sum(holds).astype(F32)

    def head_norm(vectors, gain_ref):
        mean_square = jnp.mean(vectors * vectors, axis=-1, keepdims=True)
        return (vectors * lax.rsqrt(mean_square + 1e-06) * gain_ref[...]).astype(BF16)

    pair = 2 * 3 * HD
    bank_pair = 4 * HD

    def columns_of(head):
        at = head // 2 * bank_pair + head % 2 * HD
        return (
            pl.ds(pl.multiple_of(head * HD, HD), HD),
            pl.ds(pl.multiple_of(at, HD), HD),
            pl.ds(pl.multiple_of(at + 2 * HD, HD), HD),
        )

    def project(block_at, places, after=None):
        def body(step, carry):
            columns = pl.ds(pl.multiple_of(step * pair, pair), pair)
            packed = jnp.dot(rows_buffer[block_at, :], weight[:, columns], preferred_element_type=F32)
            for half in range(2):
                at = half * 3 * HD
                head = step * 2 + half
                query_columns, key_columns, value_columns = columns_of(head)
                q = head_norm(packed[:, at : at + HD], query_gain_ref)
                k = head_norm(packed[:, at + HD : at + 2 * HD], key_gain_ref)
                v = packed[:, at + 2 * HD : at + 3 * HD].astype(BF16)
                for first, place, count in places:
                    queries[pl.ds(place, count), query_columns] = q[first : first + count]
                    bank[pl.ds(place, count), key_columns] = k[first : first + count]
                    bank[pl.ds(place, count), value_columns] = v[first : first + count]
            if after is not None:
                after(step)
            return carry

        lax.fori_loop(0, heads // 2, body, 0)

    order = ((0, 0), (0, 1), (0, 2), (1, 1), (0, 3), (1, 2), (1, 0), (1, 3))

    def quarter_of(slot, chip):
        second, quarter = order[slot]
        return second + chip * (1 - 2 * second), quarter + chip * (3 - 2 * quarter)

    def row_place(piece):
        chip, inside = piece // 6, piece % 6
        away = (chip + y) % 2
        number = inside % 3
        step = y * (2 - number) + (1 - y) * number
        return aligned(
            (1 - away) * inside * chunk + away * (6 + 2 * step + inside // 3) * chunk
        )

    half_width = width // 2

    def tile_copy(side, slot):
        second, quarter = quarter_of(slot, y)
        return pltpu.make_async_remote_copy(
            src_ref=rim_send.at[side, slot],
            dst_ref=rim.at[side, second, pl.ds(aligned(quarter * chunk), chunk), :],
            send_sem=rim_send_sem.at[side, slot],
            recv_sem=rim_recv_sem.at[side, slot],
            device_id=(right if side == 0 else left, h),
            device_id_type=MESH,
        )

    def edge_copy(side, slot):
        stage, half = slot // 2, slot % 2
        target = left + (1 - side) * (right - left)
        return pltpu.make_async_remote_copy(
            src_ref=rim_send.at[side, slot],
            dst_ref=rim_rows.at[
                pl.ds(aligned((2 * stage + c) * chunk), chunk),
                pl.ds(half * half_width, half_width),
            ],
            send_sem=rim_send_sem.at[side, slot],
            recv_sem=rim_recv_sem.at[side, slot],
            device_id=(target, cross),
            device_id_type=MESH,
        )

    def edge_pass(stage):
        here = pl.ds(aligned((2 * stage + c) * chunk), chunk)
        return pltpu.make_async_remote_copy(
            src_ref=rim_rows.at[here, :],
            dst_ref=rim_rows.at[here, :],
            send_sem=rim_pass_send.at[stage],
            recv_sem=rim_pass_recv.at[stage],
            device_id=(g, sibling),
            device_id_type=MESH,
        )

    def takes_high(side, second):
        first_tile, second_tile = send_tiles[side]
        return jnp.where(second == 0, first_tile, second_tile - 1) == 1

    def first_copy(side, slot, step):
        second, quarter = quarter_of(slot, y)
        columns = pl.ds(pl.multiple_of(step * bank_pair, bank_pair), bank_pair)
        return pltpu.make_async_remote_copy(
            src_ref=rim_send.at[side, slot, :, columns],
            dst_ref=rim.at[side, second, pl.ds(aligned(quarter * chunk), chunk), columns],
            send_sem=rim_first_send.at[side, slot, step],
            recv_sem=rim_first_recv.at[side, slot, step],
            device_id=(right if side == 0 else left, h),
            device_id_type=MESH,
        )

    def send_first_tiles(step):
        columns = pl.ds(pl.multiple_of(step * bank_pair, bank_pair), bank_pair)
        for side in range(2):
            edge = right_edge if side == 0 else left_edge

            @pl.when(edge == 0)
            def _():
                for slot in range(2):
                    second, quarter = quarter_of(slot, y)
                    low = pl.ds(aligned((4 * second + quarter) * chunk), chunk)
                    high = pl.ds(aligned((4 * second + quarter + 4) * chunk), chunk)
                    rim_send[side, slot, :, columns] = jnp.where(
                        takes_high(side, second), bank[high, columns], bank[low, columns]
                    )
                    first_copy(side, slot, step).start()

    def send_tiles_of(stage):
        for side in range(2):
            edge = right_edge if side == 0 else left_edge

            @pl.when(edge == 0)
            def _():
                for slot in (2 * stage, 2 * stage + 1):
                    second, quarter = quarter_of(slot, y)
                    low = bank[pl.ds(aligned((4 * second + quarter) * chunk), chunk), :]
                    high = bank[pl.ds(aligned((4 * second + quarter + 4) * chunk), chunk), :]
                    rim_send[side, slot] = jnp.where(takes_high(side, second), high, low)
                    tile_copy(side, slot).start()

    def send_rows_of(stage):
        for side in range(2):
            edge = right_edge if side == 0 else left_edge

            @pl.when(edge - (last_group if side == 0 else first_group) == 1)
            def _():
                second, quarter = (
                    (1 - c) * even + c * odd
                    for even, odd in zip(quarter_of(2 * stage, y), quarter_of(2 * stage + 1, y))
                )
                low = row_place(4 * second + quarter)
                high = row_place(4 * second + quarter + 4)
                for half in range(2):
                    columns = pl.ds(half * half_width, half_width)
                    rim_send[side, 2 * stage + half] = jnp.where(
                        takes_high(side, second),
                        rows_buffer[pl.ds(high, chunk), columns],
                        rows_buffer[pl.ds(low, chunk), columns],
                    )
                    edge_copy(side, 2 * stage + half).start()

    def wait_rim(slots):
        for side in range(2):
            edge = left_edge if side == 0 else right_edge

            @pl.when(edge == 0)
            def _():
                for slot in slots:
                    if slot < 2:
                        for step in range(heads // 2):
                            first_copy(side, slot, step).wait_recv()
                    else:
                        tile_copy(side, slot).wait_recv()

    def pass_edge(stage):
        @pl.when(edge_here == 1)
        def _():
            for half in range(2):
                edge_copy(edge_side, 2 * stage + half).wait_recv()
            edge_pass(stage).start()

    def project_edge(stage):
        @pl.when(edge_here == 1)
        def _():
            edge_pass(stage).wait_recv()
            places = []
            for core in range(2):
                second, quarter = quarter_of(2 * stage + core, 1 - y)
                places.append((core * chunk, second, aligned(quarter * chunk)))

            def body(step, carry):
                for head in (2 * step, 2 * step + 1):
                    columns = pl.ds(pl.multiple_of(head * 3 * HD + HD, HD), 2 * HD)
                    packed = jnp.dot(
                        rim_rows[pl.ds(2 * stage * chunk, 2 * chunk), :],
                        weight[:, columns],
                        preferred_element_type=F32,
                    )
                    k = head_norm(packed[:, :HD], key_gain_ref)
                    v = packed[:, HD:].astype(BF16)
                    _, key_columns, value_columns = columns_of(head)
                    for first, second, place in places:
                        there = pl.ds(place, chunk)
                        rim[edge_side, second, there, key_columns] = k[first : first + chunk]
                        rim[edge_side, second, there, value_columns] = v[first : first + chunk]
                return carry

            lax.fori_loop(0, heads // 2, body, 0)

    log_scale = math.log2(math.e) / math.sqrt(HD)
    triple = math.gcd(heads, 3)
    near_tile = y * 2
    far_tile = (1 - y) * 2

    def attend(q, keys, values, names):
        scores = lax.dot_general(q, keys, (((1,), (1,)), ((), ())), preferred_element_type=F32)
        weights = jnp.exp2(scores * log_scale)
        weights = jnp.concatenate(
            [weights[:, k * tile : (k + 1) * tile] * name for k, name in enumerate(names)], axis=1
        )
        total = weights[:, :HD]
        for at in range(HD, weights.shape[1], HD):
            total = total + weights[:, at : at + HD]
        return jnp.dot(weights.astype(BF16), values, preferred_element_type=F32), total

    def over_heads(work, unroll):
        def body(step, carry):
            for inner in range(unroll):
                work(step * unroll + inner)
            return carry

        lax.fori_loop(0, heads // unroll, body, 0)

    def tile_pairs(t, own, phases, fresh, head, part=None):
        start = t * tile
        if part is None:
            pieces = [pl.ds(aligned(start), tile)]
        elif part == 0:
            pieces = [pl.ds(aligned(start + at * chunk), chunk) for at in (0, 3)]
        else:
            pieces = [pl.ds(aligned(start + chunk), 2 * chunk)]

        def load(ref, columns):
            blocks = [ref[piece, columns] for piece in pieces]
            return jnp.concatenate(blocks, axis=0) if len(blocks) > 1 else blocks[0]

        def store(ref, columns, value):
            at = 0
            for piece in pieces:
                ref[piece, columns] = value[at : at + piece.size]
                at += piece.size

        columns, key_columns, value_columns = columns_of(head)
        keys, values, names = [], [], []
        for first, count in own:
            there = pl.ds(aligned(first * tile), count * tile)
            keys.append(bank[there, key_columns])
            values.append(bank[there, value_columns])
            names += [masks[t * 8 + first + k] for k in range(count)]
        for phase in phases:
            for side in range(2):
                edge = left_edge if side == 0 else right_edge
                second = (y + edge + phase) % 2
                keys.append(rim[side, second, :, key_columns])
                values.append(rim[side, second, :, value_columns])
                names.append(masks[t * 8 + 3 + 2 * side + second])
        out, total = attend(
            load(queries, columns),
            jnp.concatenate(keys, axis=0) if len(keys) > 1 else keys[0],
            jnp.concatenate(values, axis=0) if len(values) > 1 else values[0],
            names,
        )
        if not fresh:
            out = load(numerator, columns) + out
            total = load(totals, columns) + total
        if 1 not in phases:
            store(numerator, columns, out)
            store(totals, columns, total)
        else:
            slot_out = (out / jnp.sum(total, axis=-1, keepdims=True)).astype(BF16)
            kept = load(attended, columns)
            store(attended, columns, jnp.where(masks[t * 8 + 7] > 0.5, slot_out, kept))

    @pl.when(first_group + last_group == 1)
    def _():
        rim[edge_side] = jnp.zeros(rim.shape[1:], BF16)

    for load in load_weight:
        load.wait()
    load_out_weight.start()
    load_cached.start()
    for copy in to_sibling:
        copy.wait_recv()
    send_rows_of(0)
    project(
        pl.ds(0, 2 * rows), [(0, aligned(y * 2 * rows), 2 * rows)], after=send_first_tiles
    )
    passed = []
    for step in range(3):
        to_cross[step].wait_recv()
        onward = pltpu.make_async_remote_copy(
            src_ref=rows_buffer.at[pl.ds(far_place(step, c), chunk), :],
            dst_ref=rows_buffer.at[pl.ds(far_place(step, c), chunk), :],
            send_sem=pass_send.at[step],
            recv_sem=pass_recv.at[step],
            device_id=(g, sibling),
            device_id_type=MESH,
        )
        onward.start()
        passed.append(onward)
        onward.wait_recv()
        send_rows_of(step + 1)
        theirs = y * (2 - step) + (1 - y) * step
        start = (1 - y) * 2 * rows + theirs * chunk
        project(
            pl.ds(far_place(step, 0), 2 * chunk),
            [(0, aligned(start), chunk), (chunk, aligned(start + rows), chunk)],
        )
        send_tiles_of(step + 1)
        pass_edge(step)
        if step == 0:
            over_heads(lambda head: tile_pairs(near_tile, [(near_tile, 1)], (), True, head), heads)
        elif step == 1:
            over_heads(lambda head: tile_pairs(1, [(y, 2)], (), True, head), triple)
        else:
            over_heads(lambda head: tile_pairs(far_tile, [(0, 3)], (), True, head), 2)
        project_edge(step)
    wait_rim((0, 1, 2, 4))
    over_heads(lambda head: tile_pairs(far_tile, [], (0,), False, head, 0), heads)
    pass_edge(3)
    load_out_weight.wait()
    load_cached.wait()
    for copies in (to_sibling, to_cross, passed):
        for copy in copies:
            copy.wait_send()
    wait_rim((3, 5, 6, 7))
    project_edge(3)

    @pl.when(edge_here == 1)
    def _():
        for stage in range(4):
            edge_pass(stage).wait_send()

    pl.semaphore_signal(free_sem, inc=1, device_id=(g, sibling), device_id_type=MESH)
    over_heads(lambda head: tile_pairs(far_tile, [], (1,), False, head, 0), heads)
    pl.semaphore_wait(free_sem, 1)

    def half_columns(half):
        return pl.ds(half * half_width, half_width)

    sums = {}

    def project_out(slot, step, chip, chunk_at):
        owner = chip * 2 * rows + chunk_at * chunk
        both = jnp.concatenate(
            [
                attended[pl.ds(aligned(owner + core * rows), chunk), :]
                for core in (c, 1 - c)
            ],
            axis=0,
        )
        kept = pl.ds((3 * (slot // 3) + step) * chunk, chunk)
        given = pl.ds((6 + slot) * chunk, chunk)
        for half in range(2):
            columns = half_columns(half)
            part = jnp.dot(both, out_weight[:, columns], preferred_element_type=F32).astype(BF16)
            rows_buffer[given, columns] = part[chunk:]
            copy = pltpu.make_async_remote_copy(
                src_ref=rows_buffer.at[given, columns],
                dst_ref=rim_rows.at[pl.ds(slot * chunk, chunk), columns],
                send_sem=sums_send.at[slot, half],
                recv_sem=sums_recv.at[slot, half],
                device_id=(g, sibling),
                device_id_type=MESH,
            )
            copy.start()
            sums[slot, half] = copy
            rows_buffer[kept, columns] = part[:chunk]

    last = {}

    def send_last(step):
        here = pl.ds(step * chunk, chunk)
        for half in range(2):
            columns = half_columns(half)
            sums[step, half].wait_recv()
            kept = rows_buffer[here, columns].astype(F32)
            rows_buffer[here, columns] = (kept + rim_rows[here, columns].astype(F32)).astype(BF16)
            copy = pltpu.make_async_remote_copy(
                src_ref=rows_buffer.at[here, columns],
                dst_ref=cross_sums.at[step, :, columns],
                send_sem=last_send.at[step, half],
                recv_sem=last_recv.at[step, half],
                device_id=(g, cross),
                device_id_type=MESH,
            )
            copy.start()
            last[step, half] = copy

    def far_out(step):
        project_out(step, step, 1 - y, (1 - y) * (2 - step) + y * step)

    far_out(0)
    send_last(0)
    over_heads(lambda head: tile_pairs(far_tile, [], (0, 1), False, head, 1), triple)
    over_heads(lambda head: tile_pairs(1, [(far_tile, 1)], (0, 1), False, head), 2)
    far_out(1)
    far_out(2)
    send_last(1)
    send_last(2)
    over_heads(
        lambda head: tile_pairs(near_tile, [(1, 1), (far_tile, 1)], (0, 1), False, head), 2
    )
    for step in range(3):
        project_out(3 + step, step, y, y * (2 - step) + (1 - y) * step)
    stores = []
    for step in range(3):
        here = pl.ds(aligned((y * (2 - step) + (1 - y) * step) * chunk), chunk)
        own = pl.ds((3 + step) * chunk, chunk)
        for half in range(2):
            columns = half_columns(half)
            sums[3 + step, half].wait_recv()
            near_sum = rows_buffer[own, columns].astype(F32) + rim_rows[own, columns].astype(F32)
            last[step, half].wait_recv()
            total = near_sum + cross_sums[step, :, columns].astype(F32)
            latents[here, columns] = (
                latents[here, columns].astype(F32) + gate_ref[:, columns] * total
            ).astype(BF16)
            store = pltpu.make_async_copy(
                latents.at[here, columns],
                out_hbm.at[here, columns],
                local_sem.at[2 * step + half],
            )
            store.start()
            stores.append(store)
    for store in stores:
        store.wait()
    for copies in (sums, last):
        for copy in copies.values():
            copy.wait_send()
    for side in range(2):

        @pl.when((last_group if side == 0 else first_group) == 0)
        def _():
            for slot in range(2, 8):
                tile_copy(side, slot).wait_send()

        edge = right_edge if side == 0 else left_edge

        @pl.when(edge == 0)
        def _():
            for slot in range(2):
                for step in range(heads // 2):
                    first_copy(side, slot, step).wait_send()

        @pl.when(edge - (last_group if side == 0 else first_group) == 1)
        def _():
            for slot in range(2):
                edge_copy(side, slot).wait_send()


def on_device(
    latents,
    mod_shift,
    mod_scale,
    mod_gate,
    packed_weight,
    query_gain,
    key_gain,
    output_weight,
    cached,
    active_tiles,
    active_count,
    window_tiles,
    window_count,
):
    rows, width = latents.shape
    groups, tiles, window = window_tiles.shape
    share = cached.shape[1]
    heads = share // HD
    slab = cached.shape[0]
    tile = slab // tiles
    chunk = tile // 4
    assert width == 4 * share and tiles == 3 and rows == 3 * chunk and slab == 4 * rows
    anywhere = pl.BlockSpec(memory_space=pl.ANY)
    vmem = pl.BlockSpec(memory_space=pltpu.VMEM)
    smem = pl.BlockSpec(memory_space=pltpu.SMEM)
    dma = pltpu.SemaphoreType.DMA
    return pl.pallas_call(
        functools.partial(kernel, (groups, heads, tile, width, window)),
        out_shape=jax.ShapeDtypeStruct((rows, width), BF16),
        in_specs=[
            anywhere,
            vmem,
            vmem,
            vmem,
            anywhere,
            vmem,
            vmem,
            anywhere,
            anywhere,
            smem,
            smem,
            smem,
            smem,
        ],
        out_specs=anywhere,
        scratch_shapes=[
            pltpu.VMEM((rows, width), BF16),
            pltpu.VMEM((slab, width), BF16),
            pltpu.VMEM((width, 3 * share), BF16),
            pltpu.VMEM((slab, share), BF16),
            pltpu.VMEM((slab, 2 * share), BF16),
            pltpu.VMEM((2, 8, chunk, 2 * share), BF16),
            pltpu.VMEM((2, 2, tile, 2 * share), BF16),
            pltpu.VMEM((8 * chunk, width), BF16),
            pltpu.VMEM((slab, share), F32),
            pltpu.VMEM((slab, share), F32),
            pltpu.VMEM((slab, share), BF16),
            pltpu.VMEM((share, width), BF16),
            pltpu.VMEM((3, chunk, width), BF16),
            pltpu.SMEM((24,), F32),
            dma((6,)),
            dma((3,)),
            dma((3,)),
            dma((3,)),
            dma((3,)),
            dma((3,)),
            dma((3,)),
            dma((2, 8)),
            dma((2, 8)),
            dma((2, 2, heads // 2)),
            dma((2, 2, heads // 2)),
            dma((4,)),
            dma((4,)),
            dma((6, 2)),
            dma((6, 2)),
            dma((3, 2)),
            dma((3, 2)),
            pltpu.SemaphoreType.REGULAR,
        ],
        compiler_params=pltpu.CompilerParams(
            collective_id=0, has_side_effects=True, vmem_limit_bytes=VMEM_LIMIT
        ),
    )(
        latents,
        mod_shift[None],
        mod_scale[None],
        mod_gate[None],
        packed_weight,
        query_gain[None],
        key_gain[None],
        output_weight,
        cached,
        active_tiles,
        active_count,
        window_tiles.transpose(2, 1, 0),
        window_count,
    )


VMEM_LIMIT = 64 * 1024 * 1024


def solution(mesh):
    in_specs = (
        P(("frame", "head"), None),
        P(),
        P(),
        P(),
        P(None, "head"),
        P(),
        P(),
        P("head", None),
        P("frame", "head"),
        P("frame", None),
        P("frame"),
        P(),
        P("frame", None),
    )
    return jax.shard_map(
        on_device,
        mesh=mesh,
        in_specs=in_specs,
        out_specs=P(("frame", "head"), None),
        check_vma=False,
    )
```
